32 devices in a mesh: leaf: 32 (over z, y, x, core).
Axes of the slice: x: 2, y: 2, z: 4, core: 2. Of those that a mesh axis runs over, the one named last changes fastest.
Arguments:
- rhs: float32 [32768, 128], P('leaf'), may hold values from -6 to 6
- proj_bases: float32 [5, 32768, 256], P(None, 'leaf'), may hold values from -6 to 6
- corr_bases: float32 [5, 32768, 256], P(None, 'leaf'), may hold values from -0.375 to 0.375
- cores: float32 [5, 8192, 512], P(None, 'leaf'), may hold values from -0.25 to 0.25
Outputs:
- solution: float32 [32768, 128], P('leaf')
The draws below stay inside these ranges and needn't reach their ends.
All inputs are finite; a program needn't handle non-finite values.
Results may differ from the reference program's by a relative error of at most 0.00017.
Values sent between devices are 32-bit elements; how exact they have to be, the bound alone decides.
No kernel may reach another device: no remote copies, remote signals or barrier semaphores. Data moves between devices by JAX's collectives and lax.ppermute only.
A program may use at most 64 MiB of HBM per device.

```python
import jax
import jax.numpy as jnp
from jax import lax

ROWS_DEV = 1024
RANK = 256
NRHS = 128
LEVELS = 5
ROWS = 32768
CROWS = 256
N_LEAF = 32


def block_levels(rng, dims, pieces, smallest, top_value):
    def one(position, parts):
        draws = jax.random.uniform(jax.random.fold_in(jax.random.fold_in(rng, 6), position), (parts,), jnp.float32, smallest / len(pieces), top_value / len(pieces))
        return jnp.repeat(jnp.exp(draws), dims[position] // parts).reshape((-1,) + (1,) * (len(dims) - position - 1))

    gain = one(*pieces[0])
    for cut in pieces[1:]:
        gain = gain * one(*cut)
    return gain


def gaussian(key, dims, scale, bound, pieces=(), held_as=jnp.bfloat16):
    values = jax.random.normal(key, dims, jnp.float32) * scale
    if len(pieces) > 0:
        values = block_levels(key, dims, pieces, -0.22, 0.18) * values
    return jnp.clip(values, min=-bound, max=bound).astype(held_as)


def setup_inputs(seed: int = 0) -> dict:
    key_list = jax.random.split(jax.random.key(seed), 5)
    rhs = gaussian(key_list[0], (ROWS, NRHS), 1.0, 6.0, ((0, 32),), jnp.float32)
    proj_bases = gaussian(key_list[1], (LEVELS, ROWS, RANK), 1.0, 6.0, ((1, 32),), jnp.float32)
    corr_bases = gaussian(key_list[2], (LEVELS, ROWS, RANK), RANK ** -0.5, 0.375, ((1, 32),), jnp.float32)
    cores = gaussian(key_list[3], (LEVELS, N_LEAF * CROWS, 2 * RANK), (2 * RANK) ** -0.5, 0.25, ((1, 32),), jnp.float32)
    return dict(rhs=rhs, proj_bases=proj_bases, corr_bases=corr_bases, cores=cores)


def reference(rhs, proj_bases, corr_bases, cores):
    highest = lax.Precision.HIGHEST
    x = rhs.reshape(N_LEAF, ROWS_DEV, NRHS)
    for j in reversed(range(LEVELS)):
        span = N_LEAF >> j
        half = span // 2
        nodes = N_LEAF // span
        used = RANK // half
        proj = proj_bases[j].reshape(N_LEAF, ROWS_DEV, RANK)
        corr = corr_bases[j].reshape(N_LEAF, ROWS_DEV, RANK)
        part = jnp.einsum('dnr,dnk->drk', proj, x, precision=highest)
        sums = part.reshape(nodes, 2, half, RANK, NRHS).sum(axis=2)
        z_all = sums.reshape(nodes, 2 * RANK, NRHS) / jnp.sqrt(jnp.float32(ROWS_DEV * half))
        table = cores[j].reshape(N_LEAF, CROWS, 2 * RANK)[:, :used, :]
        table = table.reshape(nodes, 2, RANK, 2 * RANK)
        t_all = jnp.einsum('ncab,nbk->ncak', table, z_all, precision=highest)
        t_dev = jnp.broadcast_to(t_all.reshape(nodes, 2, 1, RANK, NRHS), (nodes, 2, half, RANK, NRHS))
        t_dev = t_dev.reshape(N_LEAF, RANK, NRHS)
        x = x - jnp.einsum('dnr,drk->dnk', corr, t_dev, precision=highest)
    return x.reshape(ROWS_DEV * N_LEAF, NRHS)
```

```python
import jax
import jax.numpy as jnp
from jax import lax
from jax.sharding import PartitionSpec as P

LEVELS = 5


def groups_of(count, size):
    return [list(range(start, start + size)) for start in range(0, count, size)]


def exchange(value, axis, mask):
    pairs = [(source, source ^ mask) for source in range(lax.axis_size(axis))]
    return lax.ppermute(value, axis, pairs)


def gather_core(mine, me, half):
    bit = 1
    while bit < half:
        partner = exchange(mine, "leaf", bit)
        mine = jnp.where(
            (me // bit) % 2 == 0,
            jnp.concatenate([mine, partner], 0),
            jnp.concatenate([partner, mine], 0),
        )
        bit *= 2
    return mine


def on_device(rhs, proj_bases, corr_bases, cores):
    high = lax.Precision.HIGH
    count = lax.axis_size("leaf")
    me = lax.axis_index("leaf")
    rows_here, width = rhs.shape
    rank = proj_bases.shape[2]
    state = rhs
    for level in reversed(range(LEVELS)):
        half = (count >> level) // 2
        core = gather_core(cores[level, : rank // half, :], me, half)
        partial = jnp.einsum("nk,nr->kr", state, proj_bases[level], precision=high)
        groups = groups_of(count, half)
        if half > 2:
            pieces = partial.reshape(half, width // half, rank)
            pieces = lax.all_to_all(pieces, "leaf", 0, 0, axis_index_groups=groups)
            partial = jnp.sum(pieces, axis=0)
        elif half == 2:
            partial = partial + exchange(partial, "leaf", 1)
        sibling = exchange(partial, "leaf", half)
        left = (me // half) % 2 == 0
        stacked = jnp.where(
            left,
            jnp.concatenate([partial, sibling], 1),
            jnp.concatenate([sibling, partial], 1),
        )
        stacked = stacked / jnp.sqrt(jnp.float32(rows_here * half))
        held = jnp.einsum("kb,ab->ka", stacked, core, precision=high)
        if half > 2:
            held = jnp.broadcast_to(held[None], (half,) + held.shape)
            held = lax.all_to_all(held, "leaf", 0, 0, axis_index_groups=groups)
            held = held.reshape(width, rank)
        state = state - jnp.einsum("na,ka->nk", corr_bases[level], held, precision=high)
    return state


def solution(mesh):
    return jax.shard_map(
        on_device,
        mesh=mesh,
        in_specs=(
            P("leaf", None),
            P(None, "leaf", None),
            P(None, "leaf", None),
            P(None, "leaf", None),
        ),
        out_specs=P("leaf", None),
        check_vma=False,
    )
```

```python
import jax
import jax.numpy as jnp
from jax import lax
from jax.sharding import PartitionSpec as P

LEVELS = 5


def groups_of(count, size):
    return [list(range(start, start + size)) for start in range(0, count, size)]


def exchange(value, axis, mask):
    pairs = [(source, source ^ mask) for source in range(lax.axis_size(axis))]
    return lax.ppermute(value, axis, pairs)


def on_device(rhs, proj_bases, corr_bases, cores):
    high = lax.Precision.HIGH
    count = lax.axis_size("leaf")
    me = lax.axis_index("leaf")
    rows_here = rhs.shape[0]
    rank = proj_bases.shape[2]
    gathered = []
    for level in range(LEVELS):
        half = (count >> level) // 2
        mine = cores[level, : rank // half, :]
        if half > 1:
            mine = lax.all_gather(
                mine, "leaf", axis_index_groups=groups_of(count, half), tiled=True
            )
        gathered.append(mine)
    state = rhs
    for level in reversed(range(LEVELS)):
        half = (count >> level) // 2
        partial = jnp.einsum("nr,nk->rk", proj_bases[level], state, precision=high)
        if half == 2:
            partial = partial + exchange(partial, "leaf", 1)
        elif half > 2:
            partial = lax.psum(partial, "leaf", axis_index_groups=groups_of(count, half))
        sibling = exchange(partial, "leaf", half)
        left = (me // half) % 2 == 0
        stacked = jnp.where(
            left,
            jnp.concatenate([partial, sibling], 0),
            jnp.concatenate([sibling, partial], 0),
        )
        stacked = stacked / jnp.sqrt(jnp.float32(rows_here * half))
        held = jnp.dot(gathered[level], stacked, precision=high)
        state = state - jnp.dot(corr_bases[level], held, precision=high)
    return state


def solution(mesh):
    return jax.shard_map(
        on_device,
        mesh=mesh,
        in_specs=(
            P("leaf", None),
            P(None, "leaf", None),
            P(None, "leaf", None),
            P(None, "leaf", None),
        ),
        out_specs=P("leaf", None),
        check_vma=False,
    )
```

```python
import jax
import jax.numpy as jnp
from jax import lax
from jax.sharding import PartitionSpec as P

LEVELS = 5
HIGH = lax.Precision.HIGH


def exchange(value, mask):
    pairs = [(source, source ^ mask) for source in range(lax.axis_size("leaf"))]
    return lax.ppermute(value, "leaf", pairs)


def pair_up(low, mine, other, axis):
    return jnp.where(
        low,
        jnp.concatenate([mine, other], axis),
        jnp.concatenate([other, mine], axis),
    )


def project(basis, state):
    return jnp.einsum("nk,nr->kr", state, basis, precision=HIGH)


def times_transposed(left, right):
    return jnp.einsum("kb,ab->ka", left, right, precision=HIGH)


def on_device(rhs, proj_bases, corr_bases, cores):
    count = lax.axis_size("leaf")
    me = lax.axis_index("leaf")
    rows_here, width = rhs.shape
    rank = proj_bases.shape[2]
    bits = [(count >> level).bit_length() - 2 for level in range(LEVELS)]
    first = LEVELS - 1

    def low(bit):
        return (me >> bit) & 1 == 0

    slices = [cores[level, : rank >> bits[level], :][None] for level in range(LEVELS)]
    for bit in range(1, max(bits)):
        users = [level for level in range(LEVELS) if bits[level] > bit]
        sizes = [slices[level].shape[0] * slices[level].shape[1] for level in users]
        bundle = jnp.concatenate([slices[level].reshape(-1, 2 * rank) for level in users], 0)
        other = exchange(bundle, 1 << bit)
        start = 0
        for level, size in zip(users, sizes):
            part = other[start : start + size].reshape(slices[level].shape)
            slices[level] = pair_up(low(bit), slices[level], part, 0)
            start += size
    users = [level for level in range(LEVELS) if bits[level] > 0]
    for level in users:
        part = exchange(slices[level], 1)
        both = jnp.where(
            low(0),
            jnp.stack([slices[level], part], 1),
            jnp.stack([part, slices[level]], 1),
        )
        slices[level] = both
    table = [piece.reshape(rank, 2 * rank) for piece in slices]

    def chip_sum(value):
        half = width // 2
        core = me & 1
        keep = lax.dynamic_slice_in_dim(value, core * half, half, 0)
        send = lax.dynamic_slice_in_dim(value, (1 - core) * half, half, 0)
        return keep + exchange(send, 1)

    def chip_gather(value):
        return pair_up(low(0), value, exchange(value, 1), 0)

    def solve(level, value):
        for bit in range(1, bits[level]):
            value = value + exchange(value, 1 << bit)
        top = bits[level]
        stacked = pair_up(low(top), value, exchange(value, 1 << top), 1)
        stacked = stacked / jnp.sqrt(jnp.float32(rows_here << top))
        return times_transposed(stacked, table[level])

    def update(level, state, held):
        return state - jnp.einsum("na,ka->nk", corr_bases[level], held, precision=HIGH)

    def cross(low_level, high_level):
        own = jnp.einsum("na,nb->ab", proj_bases[low_level], corr_bases[high_level], precision=HIGH)
        return own + exchange(own, 1)

    value = project(proj_bases[first], rhs)
    if bits[first] > 0:
        held = chip_gather(solve(first, chip_sum(value)))
    else:
        held = solve(first, value)
    state = update(first, rhs, held)
    value = chip_sum(project(proj_bases[first - 1], state))
    for level in reversed(range(first)):
        held = solve(level, value)
        if level > 0:
            ahead = chip_sum(project(proj_bases[level - 1], state))
            value = ahead - times_transposed(held, cross(level - 1, level))
        state = update(level, state, chip_gather(held))
    return state


def solution(mesh):
    return jax.shard_map(
        on_device,
        mesh=mesh,
        in_specs=(
            P("leaf", None),
            P(None, "leaf", None),
            P(None, "leaf", None),
            P(None, "leaf", None),
        ),
        out_specs=P("leaf", None),
        check_vma=False,
    )
```

```python
import functools

import jax
import jax.numpy as jnp
from jax import lax
from jax.experimental import pallas as pl
from jax.experimental.pallas import tpu as pltpu
from jax.sharding import PartitionSpec as P

LEVELS = 5
HIGH = lax.Precision.HIGH
VMEM_LIMIT = 40 * 2**20


def parts(value):
    high = value.astype(jnp.bfloat16)
    return high, (value - high.astype(jnp.float32)).astype(jnp.bfloat16)


def dot3(left, right, left_dim, right_dim):
    dims = (((left_dim,), (right_dim,)), ((), ()))

    def one(a, b):
        return lax.dot_general(a, b, dims, preferred_element_type=jnp.float32)

    return one(left[0], right[0]) + (one(left[0], right[1]) + one(left[1], right[0]))


def blocks_of(rows):
    return 4 if rows % 64 == 0 else 1


def params():
    return pltpu.CompilerParams(vmem_limit_bytes=VMEM_LIMIT)


def cost(flops, size):
    return pl.CostEstimate(flops=flops, bytes_accessed=size, transcendentals=0)


def whole(shape):
    return pl.BlockSpec(shape, lambda step: (0,) * len(shape))


def level_rows(level, block, width):
    return pl.BlockSpec((None, block, width), lambda step: (level, step, 0))


def accumulate(ref, value, step):
    @pl.when(step == 0)
    def _():
        ref[...] = value

    @pl.when(step > 0)
    def _():
        ref[...] += value


def begin(rhs, proj_bases, cores, users, first):
    rows, width = rhs.shape
    rank = proj_bases.shape[2]
    steps = blocks_of(rows)
    block = rows // steps
    head = [(level, n) for level, n, bit in users if bit == 1]
    tail = [(level, n) for level, n, bit in users if bit > 1]
    sets = [group for group in (head, tail) if group]
    count = len(head) + len(tail)

    def body(x_ref, p_ref, *refs):
        step = pl.program_id(0)
        ins, outs = refs[:count], refs[count:]

        @pl.when(step == 0)
        def _():
            place = 0
            for group, out in zip(sets, outs[1:]):
                start = 0
                for _, n in group:
                    out[start : start + n, :] = ins[place][0:n, :]
                    start += n
                    place += 1

        accumulate(outs[0], dot3(parts(x_ref[...].T), parts(p_ref[...]), 1, 0), step)

    def core_spec(level, n):
        return pl.BlockSpec((None, max(n, 8), 2 * rank), lambda step: (level, 0, 0))

    totals = [sum(n for _, n in group) for group in sets]
    shapes = [(width, rank)] + [(total, 2 * rank) for total in totals]
    out = pl.pallas_call(
        body,
        grid=(steps,),
        in_specs=[pl.BlockSpec((block, width), lambda step: (step, 0)), level_rows(first, block, rank)]
        + [core_spec(level, n) for group in sets for level, n in group],
        out_specs=[whole(shape) for shape in shapes],
        out_shape=[jax.ShapeDtypeStruct(shape, jnp.float32) for shape in shapes],
        compiler_params=params(),
        cost_estimate=cost(6 * rows * width * rank, 4 * rows * (width + rank)),
        name="begin",
    )(rhs, proj_bases, *([cores] * count))
    pieces = list(out[1:])
    return out[0], (pieces.pop(0) if head else None), (pieces.pop(0) if tail else None)


def leaf_level(rhs, own, other, cores, corr_bases, proj_bases, level, scale):
    rows, width = rhs.shape
    rank = proj_bases.shape[2]
    steps = blocks_of(rows)
    block = rows // steps

    def body(x_ref, a_ref, b_ref, c_ref, w_ref, p_ref, state_ref, y_ref, high_ref, low_ref):
        step = pl.program_id(0)

        @pl.when(step == 0)
        def _():
            left = lax.rem(lax.axis_index("leaf"), 2) == 0
            a, b = a_ref[...] * scale, b_ref[...] * scale
            z = jnp.concatenate([jnp.where(left, a, b), jnp.where(left, b, a)], 1)
            t = dot3(parts(z), parts(c_ref[...]), 1, 1)
            high_ref[...], low_ref[...] = parts(t)

        state = x_ref[...] - dot3(parts(w_ref[...]), (high_ref[...], low_ref[...]), 1, 1)
        state_ref[...] = state
        accumulate(y_ref, dot3(parts(state.T), parts(p_ref[...]), 1, 0), step)

    return pl.pallas_call(
        body,
        grid=(steps,),
        in_specs=[
            pl.BlockSpec((block, width), lambda step: (step, 0)),
            whole((width, rank)),
            whole((width, rank)),
            pl.BlockSpec((None, rank, 2 * rank), lambda step: (level, 0, 0)),
            level_rows(level, block, rank),
            level_rows(level - 1, block, rank),
        ],
        out_specs=[pl.BlockSpec((block, width), lambda step: (step, 0)), whole((width, rank))],
        out_shape=[
            jax.ShapeDtypeStruct((rows, width), jnp.float32),
            jax.ShapeDtypeStruct((width, rank), jnp.float32),
        ],
        scratch_shapes=[pltpu.VMEM((width, rank), jnp.bfloat16)] * 2,
        compiler_params=params(),
        cost_estimate=cost(12 * rows * width * rank, 4 * rows * (2 * width + 2 * rank)),
        name="leaf_level",
    )(rhs, own, other, cores, corr_bases, proj_bases)


def project_rest(state, proj_bases, levels):
    rows, width = state.shape
    rank = proj_bases.shape[2]
    steps = blocks_of(rows)
    block = rows // steps

    def body(x_ref, *refs):
        step = pl.program_id(0)
        left = parts(x_ref[...].T)
        for at, ref in enumerate(refs[:-1]):
            place = refs[-1].at[:, at * rank : (at + 1) * rank]
            accumulate(place, dot3(left, parts(ref[...]), 1, 0), step)

    shape = (width, rank * len(levels))
    return pl.pallas_call(
        body,
        grid=(steps,),
        in_specs=[pl.BlockSpec((block, width), lambda step: (step, 0))]
        + [level_rows(level, block, rank) for level in levels],
        out_specs=whole(shape),
        out_shape=jax.ShapeDtypeStruct(shape, jnp.float32),
        compiler_params=params(),
        cost_estimate=cost(6 * rows * width * shape[1], 4 * rows * (width + shape[1])),
        name="project_rest",
    )(state, *([proj_bases] * len(levels)))


def cross(corr_bases, proj_bases, upper):
    rows, rank = proj_bases.shape[1:]
    steps = blocks_of(rows)
    block = rows // steps
    lower = list(range(max(upper)))
    shapes = []
    for j in upper:
        shapes.append((rank, rank))
        if j > 1:
            shapes.append((rank, rank * (j - 1)))

    def body(*refs):
        step = pl.program_id(0)
        w_refs, p_refs = refs[: len(upper)], refs[len(upper) : len(upper) + len(lower)]
        outs = list(refs[len(upper) + len(lower) :])
        right = [parts(ref[...]) for ref in p_refs]
        for j, w_ref in zip(upper, w_refs):
            left = parts(w_ref[...].T)
            accumulate(outs.pop(0), dot3(left, right[j - 1], 1, 0), step)
            if j > 1:
                far = outs.pop(0)
                for at, i in enumerate(reversed(range(j - 1))):
                    place = far.at[:, at * rank : (at + 1) * rank]
                    accumulate(place, dot3(left, right[i], 1, 0), step)

    pairs = sum(upper)
    out = pl.pallas_call(
        body,
        grid=(steps,),
        in_specs=[level_rows(level, block, rank) for level in upper]
        + [level_rows(level, block, rank) for level in lower],
        out_specs=[whole(shape) for shape in shapes],
        out_shape=[jax.ShapeDtypeStruct(shape, jnp.float32) for shape in shapes],
        compiler_params=params(),
        cost_estimate=cost(6 * rows * rank * rank * pairs, 4 * rows * rank * 2 * len(upper)),
        name="cross",
    )(*([corr_bases] * len(upper)), *([proj_bases] * len(lower)))
    out = list(out)
    near, far = {}, {}
    for j in upper:
        near[j] = out.pop(0)
        far[j] = out.pop(0) if j > 1 else None
    return near, far


def correct(state, corr_bases, held, levels):
    rows, width = state.shape
    rank = corr_bases.shape[2]
    steps = blocks_of(rows)
    block = rows // steps
    n = len(levels)

    def body(x_ref, *refs):
        total = x_ref[...]
        for w_ref, t_ref in zip(refs[:n], refs[n : 2 * n]):
            total = total - dot3(parts(w_ref[...]), parts(t_ref[...]), 1, 1)
        refs[-1][...] = total

    tile = pl.BlockSpec((block, width), lambda step: (step, 0))
    return pl.pallas_call(
        body,
        grid=(steps,),
        in_specs=[tile] + [level_rows(level, block, rank) for level in levels] + [whole((width, rank))] * n,
        out_specs=tile,
        out_shape=jax.ShapeDtypeStruct((rows, width), jnp.float32),
        compiler_params=params(),
        cost_estimate=cost(6 * rows * width * rank * n, 4 * rows * (2 * width + rank * n)),
        name="correct",
    )(state, *([corr_bases] * n), *held)


def on_device(rhs, proj_bases, corr_bases, cores):
    count = lax.axis_size("leaf")
    me = lax.axis_index("leaf")
    rows_here, width = rhs.shape
    rank = proj_bases.shape[2]
    bits = [(count >> level).bit_length() - 2 for level in range(LEVELS)]
    chain = [level for level in reversed(range(LEVELS)) if bits[level] > 0]

    def move(value, mask, senders):
        pairs = [(source, source ^ mask) for source in range(count) if source & 1 in senders]
        return lax.ppermute(value, "leaf", pairs)

    def both(value, mask):
        return move(value, mask, (0, 1))

    def lead(value, bit):
        return move(value, 1 << bit, (1,))

    def help_(value, bit):
        return move(value, 1 << bit, (0,))

    def up(value):
        return move(value, 1, (0,))

    def down(value):
        return move(value, 1, (1,))

    def low(bit):
        return (me >> bit) & 1 == 0

    def pair_up(bit, mine, other, axis):
        return jnp.where(
            low(bit),
            jnp.concatenate([mine, other], axis),
            jnp.concatenate([other, mine], axis),
        )

    def scale(level):
        return 1.0 / float(rows_here << bits[level]) ** 0.5

    users = [(level, rank >> bits[level], bits[level]) for level in chain]
    value, head, tail = begin(rhs, proj_bases, cores, users, LEVELS - 1)

    pieces = {}
    start = 0
    for level, n, bit in users:
        if bit == 1:
            pieces[level] = head[None]
        else:
            pieces[level] = tail[start : start + n][None]
            start += n
    for bit in range(1, max(bits)):
        now = [level for level in chain if bits[level] > bit]
        bundle = jnp.concatenate([pieces[level].reshape(-1, 2 * rank) for level in now], 0)
        other = both(bundle, 1 << bit)
        start = 0
        for level in now:
            size = pieces[level].shape[0] * pieces[level].shape[1]
            part = other[start : start + size].reshape(pieces[level].shape)
            pieces[level] = pair_up(bit, pieces[level], part, 0)
            start += size
    table = {
        level: jnp.stack([up(pieces[level]), pieces[level]], 1).reshape(rank, 2 * rank) for level in chain
    }

    near, far = {}, {}
    groups = [[j] for j in chain if j > 0 and bits[j] == 1]
    groups += [[j for j in chain if j > 0 and bits[j] > 1]]
    for group in groups:
        a, b = cross(corr_bases, proj_bases, group)
        near.update(a)
        far.update(b)
    for j in chain[:-1]:
        if bits[j] == 1:
            near[j] = near[j] + up(near[j])
        else:
            total = near[j] + down(near[j])
            for bit in range(1, bits[j]):
                total = total + help_(total, bit)
            near[j] = up(total)
        if j > 1:
            far[j] = far[j] + up(far[j])

    if len(chain) < LEVELS:
        top = LEVELS - 1
        state, value = leaf_level(
            rhs, value, both(value, 1), cores, corr_bases, proj_bases, top, scale(top)
        )
    else:
        state = rhs
    rest = project_rest(state, proj_bases, chain[1:])
    value = value + up(value)
    rest = rest + up(rest)

    helds = {}
    scope = 1
    for j in chain:
        for bit in range(scope, bits[j]):
            value = value + lead(value, bit)
        stacked = pair_up(bits[j], value, lead(value, bits[j]), 1) * scale(j)
        t = jnp.einsum("kb,ab->ka", stacked, table[j], precision=HIGH)
        helds[j] = t
        if j > 0:
            ahead = rest[:, :rank]
            for bit in range(1, bits[j]):
                ahead = ahead + lead(ahead, bit)
            value = ahead - jnp.dot(t, near[j], precision=HIGH)
            if j > 1:
                rest = rest[:, rank:] - jnp.dot(t, far[j], precision=HIGH)
            scope = bits[j]
    for j in chain:
        helds[j] = jnp.where(low(0), down(helds[j]), helds[j])
    state = correct(state, corr_bases, [helds[j] for j in chain[:-1]], chain[:-1])
    return correct(state, corr_bases, [helds[0]], [0])


def solution(mesh):
    return jax.shard_map(
        on_device,
        mesh=mesh,
        in_specs=(
            P("leaf", None),
            P(None, "leaf", None),
            P(None, "leaf", None),
            P(None, "leaf", None),
        ),
        out_specs=P("leaf", None),
        check_vma=False,
    )
```

```python
import jax
import jax.numpy as jnp
from jax import lax
from jax.experimental import pallas as pl
from jax.experimental.pallas import tpu as pltpu
from jax.sharding import PartitionSpec as P

LEVELS = 5
HIGH = lax.Precision.HIGH
VMEM_LIMIT = 60 * 2**20
STEPS = 4


def parts(value):
    high = value.astype(jnp.bfloat16)
    return high, (value - high.astype(jnp.float32)).astype(jnp.bfloat16)


def left_parts(value):
    high, low = parts(value)
    return jnp.concatenate([high, high, low], 1)


def right_parts(value):
    high, low = parts(value)
    return jnp.concatenate([high, low, high], 0)


def product(left, right):
    return jnp.dot(left, right, preferred_element_type=jnp.float32)


def params():
    return pltpu.CompilerParams(vmem_limit_bytes=VMEM_LIMIT)


def cost(flops, size):
    return pl.CostEstimate(flops=flops, bytes_accessed=size, transcendentals=0)


def whole(shape):
    return pl.BlockSpec(shape, lambda step: (0,) * len(shape))


def level_rows(level, block, width):
    return pl.BlockSpec((None, block, width), lambda step: (level, step, 0))


def state_rows(block, width):
    return pl.BlockSpec((block, width), lambda step: (step, 0))


def accumulate(ref, value, step):
    @pl.when(step == 0)
    def _():
        ref[...] = value

    @pl.when(step > 0)
    def _():
        ref[...] += value


def begin(rhs, proj_bases, cores, users, first):
    rows, width = rhs.shape
    rank = proj_bases.shape[2]
    block = rows // STEPS
    head = [(level, n) for level, n, bit in users if bit == 1]
    tail = [(level, n) for level, n, bit in users if bit > 1]
    sets = [group for group in (head, tail) if group]
    count = len(head) + len(tail)

    def body(x_ref, p_ref, *refs):
        step = pl.program_id(0)
        ins, outs = refs[:count], refs[count:]

        @pl.when(step == 0)
        def _():
            place = 0
            for group, out in zip(sets, outs[1:]):
                start = 0
                for _, n in group:
                    out[start : start + n, :] = ins[place][0:n, :]
                    start += n
                    place += 1

        accumulate(outs[0], product(left_parts(p_ref[...].T), right_parts(x_ref[...])), step)

    def core_spec(level, n):
        return pl.BlockSpec((None, max(n, 8), 2 * rank), lambda step: (level, 0, 0))

    totals = [sum(n for _, n in group) for group in sets]
    shapes = [(rank, width)] + [(total, 2 * rank) for total in totals]
    out = pl.pallas_call(
        body,
        grid=(STEPS,),
        in_specs=[state_rows(block, width), level_rows(first, block, rank)]
        + [core_spec(level, n) for group in sets for level, n in group],
        out_specs=[whole(shape) for shape in shapes],
        out_shape=[jax.ShapeDtypeStruct(shape, jnp.float32) for shape in shapes],
        compiler_params=params(),
        cost_estimate=cost(6 * rows * width * rank, 4 * rows * (width + rank)),
        name="begin",
    )(rhs, proj_bases, *([cores] * count))
    pieces = list(out[1:])
    return out[0], (pieces.pop(0) if head else None), (pieces.pop(0) if tail else None)


def leaf_level(rhs, own, other, cores, corr_bases, proj_bases, level, scale):
    rows, width = rhs.shape
    rank = proj_bases.shape[2]
    block = rows // STEPS

    def body(x_ref, a_ref, b_ref, c_ref, w_ref, p_ref, state_ref, y_ref, t_ref):
        step = pl.program_id(0)

        @pl.when(step == 0)
        def _():
            left = lax.rem(lax.axis_index("leaf"), 2) == 0
            a, b = a_ref[...] * scale, b_ref[...] * scale
            z = jnp.concatenate([jnp.where(left, a, b), jnp.where(left, b, a)], 0)
            t_ref[...] = right_parts(product(left_parts(c_ref[...]), right_parts(z)))

        state = x_ref[...] - product(left_parts(w_ref[...]), t_ref[...])
        state_ref[...] = state
        accumulate(y_ref, product(left_parts(p_ref[...].T), right_parts(state)), step)

    return pl.pallas_call(
        body,
        grid=(STEPS,),
        in_specs=[
            state_rows(block, width),
            whole((rank, width)),
            whole((rank, width)),
            pl.BlockSpec((None, rank, 2 * rank), lambda step: (level, 0, 0)),
            level_rows(level, block, rank),
            level_rows(level - 1, block, rank),
        ],
        out_specs=[state_rows(block, width), whole((rank, width))],
        out_shape=[
            jax.ShapeDtypeStruct((rows, width), jnp.float32),
            jax.ShapeDtypeStruct((rank, width), jnp.float32),
        ],
        scratch_shapes=[pltpu.VMEM((3 * rank, width), jnp.bfloat16)],
        compiler_params=params(),
        cost_estimate=cost(12 * rows * width * rank, 4 * rows * (2 * width + 2 * rank)),
        name="leaf_level",
    )(rhs, own, other, cores, corr_bases, proj_bases)


def cross(state, corr_bases, proj_bases, lower, upper, after):
    rows, width = state.shape
    rank = proj_bases.shape[2]
    block = rows // STEPS

    def body(p_ref, x_ref, *refs):
        step = pl.program_id(0)
        right = jnp.concatenate([x_ref[...]] + [ref[...] for ref in refs[: len(upper)]], 1)
        accumulate(refs[-1], product(left_parts(p_ref[...].T), right_parts(right)), step)

    shape = (rank, width + rank * len(upper))
    return pl.pallas_call(
        body,
        grid=(STEPS,),
        in_specs=[level_rows(lower, block, rank), state_rows(block, width)]
        + [level_rows(level, block, rank) for level in upper]
        + [pl.BlockSpec(memory_space=pl.ANY)] * len(after),
        out_specs=whole(shape),
        out_shape=jax.ShapeDtypeStruct(shape, jnp.float32),
        compiler_params=params(),
        cost_estimate=cost(6 * rows * rank * shape[1], 4 * rows * (rank + shape[1])),
        name="cross",
    )(proj_bases, state, *([corr_bases] * len(upper)), *after)


def correct(state, corr_bases, held, levels):
    rows, width = state.shape
    rank = corr_bases.shape[2]
    block = rows // STEPS
    n = len(levels)

    def body(x_ref, *refs):
        total = x_ref[...]
        for w_ref, t_ref in zip(refs[:n], refs[n : 2 * n]):
            total = total - product(left_parts(w_ref[...]), right_parts(t_ref[...]))
        refs[-1][...] = total

    return pl.pallas_call(
        body,
        grid=(STEPS,),
        in_specs=[state_rows(block, width)]
        + [level_rows(level, block, rank) for level in levels]
        + [whole((rank, width))] * n,
        out_specs=state_rows(block, width),
        out_shape=jax.ShapeDtypeStruct((rows, width), jnp.float32),
        compiler_params=params(),
        cost_estimate=cost(6 * rows * width * rank * n, 4 * rows * (2 * width + rank * n)),
        name="correct",
    )(state, *([corr_bases] * n), *held)


def on_device(rhs, proj_bases, corr_bases, cores):
    count = lax.axis_size("leaf")
    me = lax.axis_index("leaf")
    rows_here, width = rhs.shape
    rank = proj_bases.shape[2]
    bits = [(count >> level).bit_length() - 2 for level in range(LEVELS)]
    chain = [level for level in reversed(range(LEVELS)) if bits[level] > 0]

    def both(value, bit):
        return lax.ppermute(value, "leaf", [(s, s ^ (1 << bit)) for s in range(count)])

    def lead(value, bit):
        pairs = [(s, s ^ (1 << bit) if s & 1 else s) for s in range(count)]
        return lax.ppermute(value, "leaf", pairs)

    def low(bit):
        return (me >> bit) & 1 == 0

    def pair_up(bit, mine, other, axis=0):
        return jnp.where(
            low(bit),
            jnp.concatenate([mine, other], axis),
            jnp.concatenate([other, mine], axis),
        )

    def scale(level):
        return 1.0 / float(rows_here << bits[level]) ** 0.5

    users = [(level, rank >> bits[level], bits[level]) for level in chain]
    value, head, tail = begin(rhs, proj_bases, cores, users, LEVELS - 1)
    if len(chain) < LEVELS:
        top = LEVELS - 1
        state, value = leaf_level(
            rhs, value, both(value, 0), cores, corr_bases, proj_bases, top, scale(top)
        )
    else:
        state = rhs

    ready = {chain[0]: head[None]} if head is not None else {}
    waiting = [level for level in chain if level not in ready]
    block = tail[None]
    bit = 1
    while waiting:
        block = pair_up(bit, block, both(block, bit))
        bit += 1
        done = [level for level in waiting if bits[level] == bit]
        start = 0
        for level in done:
            n = rank >> bits[level]
            ready[level] = block[:, start : start + n]
            start += n
        block = block[:, start:]
        waiting = [level for level in waiting if level not in done]
    table = {}
    for group in (chain[:2], chain[2:]):
        flat = [ready[level].reshape(-1, 2 * rank) for level in group]
        other = both(jnp.concatenate(flat, 0), 0)
        start = 0
        for level, mine in zip(group, flat):
            part = other[start : start + mine.shape[0]]
            start += mine.shape[0]
            n = rank >> bits[level]
            halves = [piece.reshape(-1, n, 2 * rank) for piece in (part, mine)]
            table[level] = jnp.stack(halves, 1).reshape(rank, 2 * rank)

    value = value + both(value, 0)
    helds = []
    after = []
    for at, j in enumerate(chain):
        if at > 0:
            products = cross(state, corr_bases, proj_bases, j, chain[:at], after)
            products = products + both(products, 0)
            value = products[:, :width]
            for k, held in enumerate(helds):
                start = width + k * rank
                value = value - jnp.dot(products[:, start : start + rank], held, precision=HIGH)
        after = [value]
        for bit in range(1, bits[j]):
            value = value + lead(value, bit)
        stacked = pair_up(bits[j], value, lead(value, bits[j])) * scale(j)
        helds.append(jnp.dot(table[j], stacked, precision=HIGH))
    early = jnp.concatenate(helds[:-1], 0)
    early = jnp.where(low(0), both(early, 0), early)
    last = jnp.where(low(0), both(helds[-1], 0), helds[-1])
    early = [early[k * rank : (k + 1) * rank] for k in range(len(chain) - 1)]
    state = correct(state, corr_bases, early, chain[:-1])
    return correct(state, corr_bases, [last], [0])


def solution(mesh):
    return jax.shard_map(
        on_device,
        mesh=mesh,
        in_specs=(
            P("leaf", None),
            P(None, "leaf", None),
            P(None, "leaf", None),
            P(None, "leaf", None),
        ),
        out_specs=P("leaf", None),
        check_vma=False,
    )
```

```python
import jax
import jax.numpy as jnp
from jax import lax
from jax.experimental import pallas as pl
from jax.experimental.pallas import tpu as pltpu
from jax.sharding import PartitionSpec as P

LEVELS = 5
HIGH = lax.Precision.HIGH


def exchange(value, mask):
    pairs = [(source, source ^ mask) for source in range(lax.axis_size("leaf"))]
    return lax.ppermute(value, "leaf", pairs)


def pair_up(low, mine, other, axis):
    return jnp.where(
        low,
        jnp.concatenate([mine, other], axis),
        jnp.concatenate([other, mine], axis),
    )


def project(basis, state):
    return jnp.einsum("nk,nr->kr", state, basis, precision=HIGH)


def times_transposed(left, right):
    return jnp.einsum("kb,ab->ka", left, right, precision=HIGH)


def pack(cores, groups, after):
    width = cores.shape[2]

    def body(core_ref, _, *refs):
        outs, sems = refs[:-1], refs[-1]
        copies = []
        for group, out in zip(groups, outs):
            start = 0
            for level, n in group:
                copies.append(
                    pltpu.make_async_copy(
                        core_ref.at[level, 0:n], out.at[start : start + n], sems.at[len(copies)]
                    )
                )
                start += n
        for copy in copies:
            copy.start()
        for copy in copies:
            copy.wait()

    anywhere = pl.BlockSpec(memory_space=pl.ANY)
    return pl.pallas_call(
        body,
        in_specs=[anywhere] * 2,
        out_specs=[anywhere] * len(groups),
        out_shape=[
            jax.ShapeDtypeStruct((sum(n for _, n in group), width), jnp.float32) for group in groups
        ],
        scratch_shapes=[pltpu.SemaphoreType.DMA((sum(len(group) for group in groups),))],
        compiler_params=pltpu.CompilerParams(vmem_limit_bytes=60 * 2**20),
        cost_estimate=pl.CostEstimate(flops=0, bytes_accessed=2**21, transcendentals=0),
        name="pack",
    )(cores, after)


def on_device(rhs, proj_bases, corr_bases, cores):
    count = lax.axis_size("leaf")
    me = lax.axis_index("leaf")
    rows_here, width = rhs.shape
    rank = proj_bases.shape[2]
    bits = [(count >> level).bit_length() - 2 for level in range(LEVELS)]
    first = LEVELS - 1

    def low(bit):
        return (me >> bit) & 1 == 0

    half_here = me & 1
    for bit in range(1, count.bit_length() - 1):
        half_here = half_here ^ ((me >> bit) & 1)

    def across(value, bit):
        return exchange(value, (1 << bit) | (1 if bit > 0 else 0))

    def gather_cores(after):
        chain = [level for level in reversed(range(LEVELS)) if bits[level] > 0]
        heads = [(level, rank >> bits[level]) for level in chain if bits[level] == 1]
        tails = [(level, rank >> bits[level]) for level in chain if bits[level] > 1]
        packed = pack(cores, [group for group in (heads, tails) if group], after)
        ready = {chain[0]: packed[0][None]} if heads else {}
        block = packed[-1][None]
        waiting = [level for level, _ in tails]
        bit = 1
        while waiting:
            block = pair_up(low(bit), block, exchange(block, 1 << bit), 0)
            bit += 1
            done = [level for level in waiting if bits[level] == bit]
            start = 0
            for level in done:
                ready[level] = block[:, start : start + (rank >> bit)]
                start += rank >> bit
            block = block[:, start:]
            waiting = [level for level in waiting if level not in done]
        table = {}
        for level in chain:
            mine = ready[level]
            part = exchange(mine, 1)
            both = jnp.where(low(0), jnp.stack([mine, part], 1), jnp.stack([part, mine], 1))
            table[level] = both.reshape(rank, 2 * rank)
        return table

    def chip_sum(value):
        half = width // 2
        keep = jnp.where(half_here == 0, value[:half], value[half:])
        send = jnp.where(half_here == 0, value[half:], value[:half])
        return keep + exchange(send, 1)

    def chip_gather(value):
        return pair_up(half_here == 0, value, exchange(value, 1), 0)

    def solve(level, value):
        for bit in range(1, bits[level]):
            value = value + across(value, bit)
        top = bits[level]
        stacked = pair_up(low(top), value, across(value, top), 1)
        stacked = stacked / jnp.sqrt(jnp.float32(rows_here << top))
        return times_transposed(stacked, table[level])

    def update(level, state, held):
        return state - jnp.einsum("na,ka->nk", corr_bases[level], held, precision=HIGH)

    def cross(low_level, high_level, after):
        left, right, _ = lax.optimization_barrier((proj_bases, corr_bases, after))
        own = jnp.einsum("na,nb->ab", left[low_level], right[high_level], precision=HIGH)
        return own + exchange(own, 1)

    value = project(proj_bases[first], rhs)
    table = gather_cores(value)
    if bits[first] > 0:
        held = chip_gather(solve(first, chip_sum(value)))
    else:
        table[first] = cores[first]
        held = solve(first, value)
    state = update(first, rhs, held)
    own = project(proj_bases[first - 1], state)
    value = chip_sum(own)
    for level in reversed(range(first)):
        start = value
        held = solve(level, value)
        if level > 0:
            ahead = chip_sum(project(proj_bases[level - 1], state))
            value = ahead - times_transposed(held, cross(level - 1, level, start))
        state = update(level, state, chip_gather(held))
    return state


def solution(mesh):
    return jax.shard_map(
        on_device,
        mesh=mesh,
        in_specs=(
            P("leaf", None),
            P(None, "leaf", None),
            P(None, "leaf", None),
            P(None, "leaf", None),
        ),
        out_specs=P("leaf", None),
        check_vma=False,
    )
```

```python
import jax
import jax.numpy as jnp
from jax import lax
from jax.experimental import pallas as pl
from jax.experimental.pallas import tpu as pltpu
from jax.sharding import PartitionSpec as P

LEVELS = 5
HIGH = lax.Precision.HIGH
IN_HBM = pl.BlockSpec(memory_space=pltpu.HBM)
IN_VMEM = pl.BlockSpec(memory_space=pltpu.VMEM)


def exchange(value, mask):
    pairs = [(source, source ^ mask) for source in range(lax.axis_size("leaf"))]
    return lax.ppermute(value, "leaf", pairs)


def tie(value, after):
    return lax.optimization_barrier((value, after))[0]


def pair_up(low, mine, other, axis):
    return jnp.where(
        low,
        jnp.concatenate([mine, other], axis),
        jnp.concatenate([other, mine], axis),
    )


def project(basis, state):
    return jnp.einsum("kn,nr->kr", state, basis, precision=HIGH)


def times_transposed(left, right):
    return jnp.einsum("kb,ab->ka", left, right, precision=HIGH)


def parts(value):
    high = value.astype(jnp.bfloat16)
    return high, (value - high.astype(jnp.float32)).astype(jnp.bfloat16)


def three_passes(left, right, dim):
    rows = left.shape[0]
    left_high, left_low = parts(left)
    right_high, right_low = parts(right)

    def one(a, b):
        return lax.dot_general(a, b, (((1,), (dim,)), ((), ())), preferred_element_type=jnp.float32)

    both = one(jnp.concatenate([left_high, left_low], 0), right_high)
    return both[:rows] + (both[rows:] + one(left_high, right_low))


def begin(rhs, proj_bases, corr_bases, cores, first, leaf_core, groups):
    rows, width = rhs.shape
    rank = proj_bases.shape[2]
    shapes = [(width, rank), (width, rows), (rows, rank), (rows, rank)]
    shapes += [(rank, 2 * rank)] if leaf_core else []
    shapes += [(sum(n for _, n in group), 2 * rank) for group in groups]

    def body(x_hbm, p_hbm, w_hbm, c_hbm, *refs):
        outs, (x_ref, p_ref, sems) = list(refs[: len(shapes)]), refs[len(shapes) :]
        q_out, state_out, w_out, p_out = outs[:4]
        rest = outs[4:]
        moves = [(x_hbm, x_ref), (p_hbm.at[first], p_ref)]
        if leaf_core:
            moves.append((c_hbm.at[first], rest.pop(0)))
        moves += [(w_hbm.at[first], w_out), (p_hbm.at[first - 1], p_out)]
        for group, out in zip(groups, rest):
            start = 0
            for level, n in group:
                moves.append((c_hbm.at[level, 0:n], out.at[start : start + n]))
                start += n
        copies = [pltpu.make_async_copy(a, b, sems.at[at]) for at, (a, b) in enumerate(moves)]
        for copy in copies:
            copy.start()
        copies[0].wait()
        state = x_ref[...].T
        state_out[...] = state
        copies[1].wait()
        q_out[...] = three_passes(state, p_ref[...], 0)
        for copy in copies[2:]:
            copy.wait()

    count = 4 + (1 if leaf_core else 0) + sum(len(group) for group in groups)
    return pl.pallas_call(
        body,
        in_specs=[IN_HBM] * 4,
        out_specs=[IN_VMEM] * len(shapes),
        out_shape=[pltpu.VMEM(shape, jnp.float32) for shape in shapes],
        scratch_shapes=[
            pltpu.VMEM((rows, width), jnp.float32),
            pltpu.VMEM((rows, rank), jnp.float32),
            pltpu.SemaphoreType.DMA((count,)),
        ],
        compiler_params=pltpu.CompilerParams(vmem_limit_bytes=52 * 2**20),
        cost_estimate=pl.CostEstimate(
            flops=6 * rows * width * rank, bytes_accessed=2**22, transcendentals=0
        ),
        name="begin",
    )(rhs, proj_bases, corr_bases, cores)


def finish(state, corr, held):
    width, rows = state.shape

    def body(x_ref, w_ref, t_ref, out_ref):
        out_ref[...] = (x_ref[...] - three_passes(t_ref[...], w_ref[...], 1)).T

    return pl.pallas_call(
        body,
        in_specs=[IN_VMEM] * 3,
        out_specs=IN_VMEM,
        out_shape=jax.ShapeDtypeStruct((rows, width), jnp.float32),
        compiler_params=pltpu.CompilerParams(vmem_limit_bytes=24 * 2**20),
        cost_estimate=pl.CostEstimate(
            flops=6 * rows * width * corr.shape[1], bytes_accessed=2**21, transcendentals=0
        ),
        name="finish",
    )(state, corr, held)


def on_device(rhs, proj_bases, corr_bases, cores):
    count = lax.axis_size("leaf")
    me = lax.axis_index("leaf")
    rows_here, width = rhs.shape
    rank = proj_bases.shape[2]
    bits = [(count >> level).bit_length() - 2 for level in range(LEVELS)]
    first = LEVELS - 1
    chain = [level for level in reversed(range(LEVELS)) if bits[level] > 0]

    def low(bit):
        return (me >> bit) & 1 == 0

    parity = me & 1
    for bit in range(1, count.bit_length() - 1):
        parity = parity ^ ((me >> bit) & 1)
    upper = parity == 0

    def across(value, bit):
        return exchange(value, (1 << bit) | (1 if bit > 0 else 0))

    def chip_sum(value):
        half = width // 2
        keep = jnp.where(upper, value[:half], value[half:])
        send = jnp.where(upper, value[half:], value[:half])
        return keep + exchange(send, 1)

    def chip_gather(value):
        return pair_up(upper, value, exchange(value, 1), 0)

    heads = [(level, rank >> bits[level]) for level in chain if bits[level] == 1]
    tails = [(level, rank >> bits[level]) for level in chain if bits[level] > 1]
    groups = [group for group in (heads, tails) if group]
    leaf_core = bits[first] == 0
    value, state, top_corr, next_proj, *fetched = begin(
        rhs, proj_bases, corr_bases, cores, first, leaf_core, groups
    )

    table = {}
    if leaf_core:
        table[first] = fetched.pop(0)

    def finish_table(level, mine):
        part = exchange(mine, 1)
        both = jnp.where(low(0), jnp.stack([mine, part], 1), jnp.stack([part, mine], 1))
        table[level] = both.reshape(rank, 2 * rank)

    block = fetched[-1][None]
    coming = None
    waiting = [level for level, _ in tails]
    gather_bit = 1

    def send(after):
        nonlocal coming
        if waiting and coming is None:
            coming = exchange(tie(block, after), 1 << gather_bit)

    def join(after):
        nonlocal block, coming, waiting, gather_bit
        block = pair_up(low(gather_bit), block, tie(coming, after), 0)
        coming = None
        gather_bit += 1
        done = [level for level in waiting if bits[level] == gather_bit]
        waiting = [level for level in waiting if level not in done]
        start = 0
        for level in done:
            finish_table(level, block[:, start : start + (rank >> gather_bit)])
            start += rank >> gather_bit
        block = block[:, start:]

    def solve(level, value):
        for bit in range(1, bits[level]):
            value = value + across(value, bit)
        while level not in table:
            send(value)
            join(value)
        top = bits[level]
        stacked = pair_up(low(top), value, across(value, top), 1)
        stacked = stacked / jnp.sqrt(jnp.float32(rows_here << top))
        return times_transposed(stacked, table[level])

    def update(corr, state, held):
        return state - jnp.einsum("ka,na->kn", held, corr, precision=HIGH)

    if leaf_core:
        top = pair_up(low(0), value, exchange(value, 1), 1)
        top = top / jnp.sqrt(jnp.float32(rows_here))
        held = times_transposed(top, table[first])
    else:
        held = chip_gather(solve(first, chip_sum(value)))
    state = update(top_corr, state, held)
    value = chip_sum(project(next_proj, state))
    if heads:
        finish_table(heads[0][0], tie(fetched[0], value)[None])
    for level in reversed(range(first)):
        start = value
        held = solve(level, value)
        if level > 0:
            projs, corrs = lax.optimization_barrier((proj_bases, corr_bases, start))[:2]
            ahead = chip_sum(project(projs[level - 1], state))
            own = jnp.einsum("na,nb->ab", projs[level - 1], corrs[level], precision=HIGH)
            if level == first - 1:
                send(own)
            value = ahead - times_transposed(held, own + exchange(own, 1))
            send(value)
            state = update(corrs[level], state, chip_gather(held))
    return finish(state, corr_bases[0], chip_gather(held))


def solution(mesh):
    return jax.shard_map(
        on_device,
        mesh=mesh,
        in_specs=(
            P("leaf", None),
            P(None, "leaf", None),
            P(None, "leaf", None),
            P(None, "leaf", None),
        ),
        out_specs=P("leaf", None),
        check_vma=False,
    )
```

```python
import jax
import jax.numpy as jnp
from jax import lax
from jax.experimental import pallas as pl
from jax.experimental.pallas import tpu as pltpu
from jax.sharding import PartitionSpec as P

LEVELS = 5
HIGH = lax.Precision.HIGH
IN_HBM = pl.BlockSpec(memory_space=pltpu.HBM)
IN_VMEM = pl.BlockSpec(memory_space=pltpu.VMEM)


def exchange(value, mask):
    pairs = [(source, source ^ mask) for source in range(lax.axis_size("leaf"))]
    return lax.ppermute(value, "leaf", pairs)


def tie(value, after):
    return lax.optimization_barrier((value, after))[0]


def pair_up(low, mine, other, axis):
    return jnp.where(
        low,
        jnp.concatenate([mine, other], axis),
        jnp.concatenate([other, mine], axis),
    )


def project(basis, state):
    return jnp.einsum("kn,nr->kr", state, basis, precision=HIGH)


def times_transposed(left, right):
    return jnp.einsum("kb,ab->ka", left, right, precision=HIGH)


def parts(value):
    high = value.astype(jnp.bfloat16)
    return high, (value - high.astype(jnp.float32)).astype(jnp.bfloat16)


def three_passes(left, right, dim):
    rows = left.shape[0]
    left_high, left_low = parts(left)
    right_high, right_low = parts(right)

    def one(a, b):
        return lax.dot_general(a, b, (((1,), (dim,)), ((), ())), preferred_element_type=jnp.float32)

    both = one(jnp.concatenate([left_high, left_low], 0), right_high)
    return both[:rows] + (both[rows:] + one(left_high, right_low))


def begin(rhs, proj_bases, corr_bases, cores, first, leaf_core, groups):
    rows, width = rhs.shape
    rank = proj_bases.shape[2]
    shapes = [(width, rank), (width, rows)] + [(rows, rank)] * 4
    shapes += [(rank, 2 * rank)] if leaf_core else []
    shapes += [(sum(n for _, n in group), 2 * rank) for group in groups]

    def body(x_hbm, p_hbm, w_hbm, c_hbm, *refs):
        outs, (x_ref, p_ref, sems) = list(refs[: len(shapes)]), refs[len(shapes) :]
        q_out, state_out, w_out, p_out, w_next, p_next = outs[:6]
        rest = outs[6:]
        moves = [(x_hbm, x_ref), (p_hbm.at[first], p_ref)]
        if leaf_core:
            moves.append((c_hbm.at[first], rest.pop(0)))
        moves += [(w_hbm.at[first], w_out), (p_hbm.at[first - 1], p_out)]
        for group, out in zip(groups, rest):
            start = 0
            for level, n in group:
                moves.append((c_hbm.at[level, 0:n], out.at[start : start + n]))
                start += n
        moves += [(w_hbm.at[first - 1], w_next), (p_hbm.at[first - 2], p_next)]
        copies = [pltpu.make_async_copy(a, b, sems.at[at]) for at, (a, b) in enumerate(moves)]
        for copy in copies:
            copy.start()
        copies[0].wait()
        state = x_ref[...].T
        state_out[...] = state
        copies[1].wait()
        q_out[...] = three_passes(state, p_ref[...], 0)
        for copy in copies[2:]:
            copy.wait()

    count = 6 + (1 if leaf_core else 0) + sum(len(group) for group in groups)
    return pl.pallas_call(
        body,
        in_specs=[IN_HBM] * 4,
        out_specs=[IN_VMEM] * len(shapes),
        out_shape=[pltpu.VMEM(shape, jnp.float32) for shape in shapes],
        scratch_shapes=[
            pltpu.VMEM((rows, width), jnp.float32),
            pltpu.VMEM((rows, rank), jnp.float32),
            pltpu.SemaphoreType.DMA((count,)),
        ],
        compiler_params=pltpu.CompilerParams(vmem_limit_bytes=52 * 2**20),
        cost_estimate=pl.CostEstimate(
            flops=6 * rows * width * rank, bytes_accessed=2**22, transcendentals=0
        ),
        name="begin",
    )(rhs, proj_bases, corr_bases, cores)


def fetch(corr_bases, after):
    rows, rank = corr_bases.shape[1:]

    def body(w_hbm, _, one, zero, sems):
        copies = [
            pltpu.make_async_copy(w_hbm.at[level], out, sems.at[level])
            for level, out in enumerate((zero, one))
        ]
        for copy in copies:
            copy.start()
        for copy in copies:
            copy.wait()

    return pl.pallas_call(
        body,
        in_specs=[IN_HBM, pl.BlockSpec(memory_space=pl.ANY)],
        out_specs=[IN_VMEM] * 2,
        out_shape=[pltpu.VMEM((rows, rank), jnp.float32)] * 2,
        scratch_shapes=[pltpu.SemaphoreType.DMA((2,))],
        compiler_params=pltpu.CompilerParams(vmem_limit_bytes=32 * 2**20),
        cost_estimate=pl.CostEstimate(flops=0, bytes_accessed=2**22, transcendentals=0),
        name="fetch",
    )(corr_bases, after)


def finish(state, corr, held):
    width, rows = state.shape

    def body(x_ref, w_ref, t_ref, out_ref):
        out_ref[...] = (x_ref[...] - three_passes(t_ref[...], w_ref[...], 1)).T

    return pl.pallas_call(
        body,
        in_specs=[IN_VMEM] * 3,
        out_specs=IN_VMEM,
        out_shape=jax.ShapeDtypeStruct((rows, width), jnp.float32),
        compiler_params=pltpu.CompilerParams(vmem_limit_bytes=24 * 2**20),
        cost_estimate=pl.CostEstimate(
            flops=6 * rows * width * corr.shape[1], bytes_accessed=2**21, transcendentals=0
        ),
        name="finish",
    )(state, corr, held)


def on_device(rhs, proj_bases, corr_bases, cores):
    count = lax.axis_size("leaf")
    me = lax.axis_index("leaf")
    rows_here, width = rhs.shape
    rank = proj_bases.shape[2]
    bits = [(count >> level).bit_length() - 2 for level in range(LEVELS)]
    first = LEVELS - 1
    chain = [level for level in reversed(range(LEVELS)) if bits[level] > 0]

    def low(bit):
        return (me >> bit) & 1 == 0

    parity = me & 1
    for bit in range(1, count.bit_length() - 1):
        parity = parity ^ ((me >> bit) & 1)
    upper = parity == 0

    def across(value, bit):
        return exchange(value, (1 << bit) | (1 if bit > 0 else 0))

    def chip_sum(value):
        half = width // 2
        keep = jnp.where(upper, value[:half], value[half:])
        send = jnp.where(upper, value[half:], value[:half])
        return keep + exchange(send, 1)

    def chip_gather(value):
        return pair_up(upper, value, exchange(value, 1), 0)

    heads = [(level, rank >> bits[level]) for level in chain if bits[level] == 1]
    tails = [(level, rank >> bits[level]) for level in chain if bits[level] > 1]
    groups = [group for group in (heads, tails) if group]
    leaf_core = bits[first] == 0
    value, state, top_corr, next_proj, next_corr, after_proj, *fetched = begin(
        rhs, proj_bases, corr_bases, cores, first, leaf_core, groups
    )

    table = {}
    if leaf_core:
        table[first] = fetched.pop(0)

    def finish_table(level, mine):
        part = exchange(mine, 1)
        both = jnp.where(low(0), jnp.stack([mine, part], 1), jnp.stack([part, mine], 1))
        table[level] = both.reshape(rank, 2 * rank)

    def gather_steps():
        block = fetched[-1][None]
        waiting = [level for level, _ in tails]
        bit = 1
        coming = exchange(block, 2)
        while True:
            after = yield
            block = pair_up(low(bit), block, tie(coming, after), 0)
            bit += 1
            after = yield
            rows = rank >> bit
            for level in [level for level in waiting if bits[level] == bit]:
                finish_table(level, tie(block[:, :rows], after))
                block = block[:, rows:]
            waiting = [level for level in waiting if bits[level] > bit]
            if waiting:
                coming = exchange(tie(block, after), 1 << bit)
            else:
                return

    steps = gather_steps()
    next(steps)

    def step(after):
        try:
            steps.send(after)
        except StopIteration:
            pass

    def solve(level, value, ahead_of):
        top = bits[level]
        for bit in range(1, top):
            value = ahead_of.get(bit, lambda v: v)(value)
            value = value + across(value, bit)
        while level not in table:
            step(value)
        if top > 1:
            step(value)
            step(value)
        value = ahead_of.get(top, lambda v: v)(value)
        stacked = pair_up(low(top), value, across(value, top), 1)
        stacked = stacked / jnp.sqrt(jnp.float32(rows_here << top))
        return times_transposed(stacked, table[level])

    def update(corr, state, held):
        return state - jnp.einsum("ka,na->kn", held, corr, precision=HIGH)

    if leaf_core:
        top = pair_up(low(0), value, exchange(value, 1), 1)
        top = top / jnp.sqrt(jnp.float32(rows_here))
        held = times_transposed(top, table[first])
    else:
        held = chip_gather(solve(first, chip_sum(value), {}))
    state = update(top_corr, state, held)
    value = chip_sum(project(next_proj, state))
    if heads:
        step(value)
        finish_table(heads[0][0], tie(fetched[0], value)[None])
    for level in reversed(range(1, first)):
        start = value
        held = solve(level, value, {})
        if level == first - 1:
            proj, corr = tie(after_proj, start), tie(next_corr, start)
        else:
            projs, corrs = lax.optimization_barrier((proj_bases, corr_bases, start))[:2]
            proj, corr = projs[level - 1], corrs[level]
        ahead = chip_sum(project(proj, state))
        own = jnp.einsum("na,nb->ab", proj, corr, precision=HIGH)
        if heads and level == first - 1:
            step(own)
        value = ahead - times_transposed(held, own + exchange(own, 1))
        if level > 1:
            state = update(corr, state, chip_gather(held))
    one_corr, zero_corr = fetch(corr_bases, value)
    state = update(one_corr, state, chip_gather(held))
    ahead_of = {
        bits[0] - 1: lambda v: lax.optimization_barrier((v, one_corr, zero_corr))[0],
        bits[0]: lambda v: tie(v, state),
    }
    held = solve(0, value, ahead_of)
    return finish(state, zero_corr, chip_gather(held))


def solution(mesh):
    return jax.shard_map(
        on_device,
        mesh=mesh,
        in_specs=(
            P("leaf", None),
            P(None, "leaf", None),
            P(None, "leaf", None),
            P(None, "leaf", None),
        ),
        out_specs=P("leaf", None),
        check_vma=False,
    )
```

```python
import jax
import jax.numpy as jnp
from jax import lax
from jax.experimental import pallas as pl
from jax.experimental.pallas import tpu as pltpu
from jax.sharding import PartitionSpec as P

LEVELS = 5
HIGH = lax.Precision.HIGH
IN_HBM = pl.BlockSpec(memory_space=pltpu.HBM)
IN_VMEM = pl.BlockSpec(memory_space=pltpu.VMEM)


def exchange(value, mask):
    pairs = [(source, source ^ mask) for source in range(lax.axis_size("leaf"))]
    return lax.ppermute(value, "leaf", pairs)


def tie(value, after):
    return lax.optimization_barrier((value, after))[0]


def pair_up(low, mine, other, axis):
    return jnp.where(
        low,
        jnp.concatenate([mine, other], axis),
        jnp.concatenate([other, mine], axis),
    )


def project(basis, state):
    return jnp.einsum("kn,nr->kr", state, basis, precision=HIGH)


def times_transposed(left, right):
    return jnp.einsum("kb,ab->ka", left, right, precision=HIGH)


def parts(value):
    high = value.astype(jnp.bfloat16)
    return high, (value - high.astype(jnp.float32)).astype(jnp.bfloat16)


def three_passes(left, right, dim):
    rows = left.shape[0]
    left_high, left_low = parts(left)
    right_high, right_low = parts(right)

    def one(a, b):
        return lax.dot_general(a, b, (((1,), (dim,)), ((), ())), preferred_element_type=jnp.float32)

    both = one(jnp.concatenate([left_high, left_low], 0), right_high)
    return both[:rows] + (both[rows:] + one(left_high, right_low))


def begin(rhs, proj_bases, corr_bases, cores, first, leaf_core, groups):
    rows, width = rhs.shape
    rank = proj_bases.shape[2]
    shapes = [(width, rank), (width, rows)] + [(rows, rank)] * 2
    shapes += [(rank, 2 * rank)] if leaf_core else []
    shapes += [(sum(n for _, n in group), 2 * rank) for group in groups]

    def body(x_hbm, p_hbm, w_hbm, c_hbm, *refs):
        outs, (x_ref, p_ref, sems) = list(refs[: len(shapes)]), refs[len(shapes) :]
        q_out, state_out, w_out, p_out = outs[:4]
        rest = outs[4:]
        moves = [(x_hbm, x_ref), (p_hbm.at[first], p_ref)]
        if leaf_core:
            moves.append((c_hbm.at[first], rest.pop(0)))
        moves += [(w_hbm.at[first], w_out), (p_hbm.at[first - 1], p_out)]
        for group, out in zip(groups, rest):
            start = 0
            for level, n in group:
                moves.append((c_hbm.at[level, 0:n], out.at[start : start + n]))
                start += n
        copies = [pltpu.make_async_copy(a, b, sems.at[at]) for at, (a, b) in enumerate(moves)]
        for copy in copies:
            copy.start()
        copies[0].wait()
        state = x_ref[...].T
        state_out[...] = state
        copies[1].wait()
        q_out[...] = three_passes(state, p_ref[...], 0)
        for copy in copies[2:]:
            copy.wait()

    count = 4 + (1 if leaf_core else 0) + sum(len(group) for group in groups)
    return pl.pallas_call(
        body,
        in_specs=[IN_HBM] * 4,
        out_specs=[IN_VMEM] * len(shapes),
        out_shape=[pltpu.VMEM(shape, jnp.float32) for shape in shapes],
        scratch_shapes=[
            pltpu.VMEM((rows, width), jnp.float32),
            pltpu.VMEM((rows, rank), jnp.float32),
            pltpu.SemaphoreType.DMA((count,)),
        ],
        compiler_params=pltpu.CompilerParams(vmem_limit_bytes=52 * 2**20),
        cost_estimate=pl.CostEstimate(
            flops=6 * rows * width * rank, bytes_accessed=2**22, transcendentals=0
        ),
        name="begin",
    )(rhs, proj_bases, corr_bases, cores)


def finish(state, corr, held):
    width, rows = state.shape

    def body(x_ref, w_ref, t_ref, out_ref):
        out_ref[...] = (x_ref[...] - three_passes(t_ref[...], w_ref[...], 1)).T

    return pl.pallas_call(
        body,
        in_specs=[IN_VMEM] * 3,
        out_specs=IN_VMEM,
        out_shape=jax.ShapeDtypeStruct((rows, width), jnp.float32),
        compiler_params=pltpu.CompilerParams(vmem_limit_bytes=16 * 2**20),
        cost_estimate=pl.CostEstimate(
            flops=6 * rows * width * corr.shape[1], bytes_accessed=2**21, transcendentals=0
        ),
        name="finish",
    )(state, corr, held)


def on_device(rhs, proj_bases, corr_bases, cores):
    count = lax.axis_size("leaf")
    me = lax.axis_index("leaf")
    rows_here, width = rhs.shape
    rank = proj_bases.shape[2]
    bits = [(count >> level).bit_length() - 2 for level in range(LEVELS)]
    first = LEVELS - 1
    chain = [level for level in reversed(range(LEVELS)) if bits[level] > 0]

    def low(bit):
        return (me >> bit) & 1 == 0

    parity = me & 1
    for bit in range(1, count.bit_length() - 1):
        parity = parity ^ ((me >> bit) & 1)
    upper = parity == 0

    def across(value, bit):
        return exchange(value, (1 << bit) | (1 if bit > 0 else 0))

    def chip_sum(value):
        half = width // 2
        keep = jnp.where(upper, value[:half], value[half:])
        send = jnp.where(upper, value[half:], value[:half])
        return keep + exchange(send, 1)

    def chip_gather(value):
        return pair_up(upper, value, exchange(value, 1), 0)

    heads = [(level, rank >> bits[level]) for level in chain if bits[level] == 1]
    tails = [(level, rank >> bits[level]) for level in chain if bits[level] > 1]
    groups = [group for group in (heads, tails) if group]
    leaf_core = bits[first] == 0
    value, state, top_corr, next_proj, *fetched = begin(
        rhs, proj_bases, corr_bases, cores, first, leaf_core, groups
    )

    table = {}
    if leaf_core:
        table[first] = fetched.pop(0)

    def finish_table(level, mine):
        part = exchange(mine, 1)
        both = jnp.where(low(0), jnp.stack([mine, part], 1), jnp.stack([part, mine], 1))
        table[level] = both.reshape(rank, 2 * rank)

    def gather_steps():
        block = fetched[-1][None]
        waiting = [level for level, _ in tails]
        bit = 1
        coming = exchange(block, 2)
        while True:
            after = yield
            block = pair_up(low(bit), block, tie(coming, after), 0)
            bit += 1
            after = yield
            rows = rank >> bit
            for level in [level for level in waiting if bits[level] == bit]:
                finish_table(level, tie(block[:, :rows], after))
                block = block[:, rows:]
            waiting = [level for level in waiting if bits[level] > bit]
            if waiting:
                coming = exchange(tie(block, after), 1 << bit)
            else:
                return

    steps = gather_steps()
    next(steps)

    def step(after):
        try:
            steps.send(after)
        except StopIteration:
            pass

    def solve(level, value, ahead_of):
        top = bits[level]
        for bit in range(1, top):
            value = ahead_of.get(bit, lambda v: v)(value)
            value = value + across(value, bit)
        while level not in table:
            step(value)
        if top > 1:
            step(value)
            step(value)
        value = ahead_of.get(top, lambda v: v)(value)
        stacked = pair_up(low(top), value, across(value, top), 1)
        stacked = stacked / jnp.sqrt(jnp.float32(rows_here << top))
        return times_transposed(stacked, table[level])

    def update(corr, state, held):
        return state - jnp.einsum("ka,na->kn", held, corr, precision=HIGH)

    if leaf_core:
        top = pair_up(low(0), value, exchange(value, 1), 1)
        top = top / jnp.sqrt(jnp.float32(rows_here))
        held = times_transposed(top, table[first])
    else:
        held = chip_gather(solve(first, chip_sum(value), {}))
    state = update(top_corr, state, held)
    value = chip_sum(project(next_proj, state))
    if heads:
        step(value)
        finish_table(heads[0][0], tie(fetched[0], value)[None])
    for level in reversed(range(1, first)):
        start = value
        held = solve(level, value, {})
        projs, corrs = lax.optimization_barrier((proj_bases, corr_bases, start))[:2]
        proj, corr = projs[level - 1], corrs[level]
        ahead = chip_sum(project(proj, state))
        own = jnp.einsum("na,nb->ab", proj, corr, precision=HIGH)
        if heads and level == first - 1:
            step(own)
        value = ahead - times_transposed(held, own + exchange(own, 1))
        if level > 1:
            state = update(corr, state, chip_gather(held))
    last_corrs = tie(corr_bases, value)
    one_corr, zero_corr = last_corrs[1], last_corrs[0]
    state = update(one_corr, state, chip_gather(held))
    ahead_of = {
        bits[0] - 1: lambda v: tie(v, zero_corr),
        bits[0]: lambda v: tie(v, state),
    }
    held = solve(0, value, ahead_of)
    return finish(state, zero_corr, chip_gather(held))


def solution(mesh):
    return jax.shard_map(
        on_device,
        mesh=mesh,
        in_specs=(
            P("leaf", None),
            P(None, "leaf", None),
            P(None, "leaf", None),
            P(None, "leaf", None),
        ),
        out_specs=P("leaf", None),
        check_vma=False,
    )
```

```python
import jax
import jax.numpy as jnp
from jax import lax
from jax.experimental import pallas as pl
from jax.experimental.pallas import tpu as pltpu
from jax.sharding import PartitionSpec as P

LEVELS = 5
HIGH = lax.Precision.HIGH
IN_VMEM = pl.BlockSpec(memory_space=pltpu.VMEM)


def exchange(value, mask):
    pairs = [(source, source ^ mask) for source in range(lax.axis_size("leaf"))]
    return lax.ppermute(value, "leaf", pairs)


def tie(value, after):
    return lax.optimization_barrier((value, after))[0]


def pair_up(low, mine, other, axis):
    return jnp.where(
        low,
        jnp.concatenate([mine, other], axis),
        jnp.concatenate([other, mine], axis),
    )


def project(basis, state):
    return jnp.einsum("kn,nr->kr", state, basis, precision=HIGH)


def times_transposed(left, right):
    return jnp.einsum("kb,ab->ka", left, right, precision=HIGH)


def parts(value):
    high = value.astype(jnp.bfloat16)
    return high, (value - high.astype(jnp.float32)).astype(jnp.bfloat16)


def three_passes(left, right, dim):
    rows = left.shape[0]
    left_high, left_low = parts(left)
    right_high, right_low = parts(right)

    def one(a, b):
        return lax.dot_general(a, b, (((1,), (dim,)), ((), ())), preferred_element_type=jnp.float32)

    both = one(jnp.concatenate([left_high, left_low], 0), right_high)
    return both[:rows] + (both[rows:] + one(left_high, right_low))


def pack(cores, groups, after):
    width = cores.shape[2]

    def body(core_ref, _, *outs):
        for group, out in zip(groups, outs):
            start = 0
            for level, n in group:
                out[start : start + n, :] = core_ref[level, 0:n, :]
                start += n

    return pl.pallas_call(
        body,
        in_specs=[IN_VMEM, pl.BlockSpec(memory_space=pl.ANY)],
        out_specs=[IN_VMEM] * len(groups),
        out_shape=[
            jax.ShapeDtypeStruct((sum(n for _, n in group), width), jnp.float32) for group in groups
        ],
        compiler_params=pltpu.CompilerParams(vmem_limit_bytes=16 * 2**20),
        cost_estimate=pl.CostEstimate(flops=0, bytes_accessed=2**20, transcendentals=0),
        name="pack",
    )(cores, after)


def finish(state, corr, held):
    width, rows = state.shape

    def body(x_ref, w_ref, t_ref, out_ref):
        out_ref[...] = (x_ref[...] - three_passes(t_ref[...], w_ref[...], 1)).T

    return pl.pallas_call(
        body,
        in_specs=[IN_VMEM] * 3,
        out_specs=IN_VMEM,
        out_shape=jax.ShapeDtypeStruct((rows, width), jnp.float32),
        compiler_params=pltpu.CompilerParams(vmem_limit_bytes=16 * 2**20),
        cost_estimate=pl.CostEstimate(
            flops=6 * rows * width * corr.shape[1], bytes_accessed=2**21, transcendentals=0
        ),
        name="finish",
    )(state, corr, held)


def on_device(rhs, proj_bases, corr_bases, cores):
    count = lax.axis_size("leaf")
    me = lax.axis_index("leaf")
    rows_here, width = rhs.shape
    rank = proj_bases.shape[2]
    bits = [(count >> level).bit_length() - 2 for level in range(LEVELS)]
    first = LEVELS - 1
    chain = [level for level in reversed(range(LEVELS)) if bits[level] > 0]

    def low(bit):
        return (me >> bit) & 1 == 0

    parity = me & 1
    for bit in range(1, count.bit_length() - 1):
        parity = parity ^ ((me >> bit) & 1)
    upper = parity == 0

    def across(value, bit):
        return exchange(value, (1 << bit) | (1 if bit > 0 else 0))

    def chip_sum(value):
        half = width // 2
        keep = jnp.where(upper, value[:half], value[half:])
        send = jnp.where(upper, value[half:], value[:half])
        return keep + exchange(send, 1)

    def chip_gather(value):
        return pair_up(upper, value, exchange(value, 1), 0)

    heads = [(level, rank >> bits[level]) for level in chain if bits[level] == 1]
    tails = [(level, rank >> bits[level]) for level in chain if bits[level] > 1]
    groups = [group for group in (heads, tails) if group]
    leaf_core = bits[first] == 0
    value = jnp.einsum("nk,nr->kr", rhs, proj_bases[first], precision=HIGH)
    state = rhs.T
    fetched = pack(cores, groups, value)

    table = {}
    if leaf_core:
        table[first] = cores[first]

    def finish_table(level, mine):
        part = exchange(mine, 1)
        both = jnp.where(low(0), jnp.stack([mine, part], 1), jnp.stack([part, mine], 1))
        table[level] = both.reshape(rank, 2 * rank)

    def gather_steps():
        block = fetched[-1][None]
        waiting = [level for level, _ in tails]
        bit = 1
        coming = exchange(block, 2)
        while True:
            after = yield
            block = pair_up(low(bit), block, tie(coming, after), 0)
            bit += 1
            after = yield
            rows = rank >> bit
            for level in [level for level in waiting if bits[level] == bit]:
                finish_table(level, tie(block[:, :rows], after))
                block = block[:, rows:]
            waiting = [level for level in waiting if bits[level] > bit]
            if waiting:
                coming = exchange(tie(block, after), 1 << bit)
            else:
                return

    steps = gather_steps()
    next(steps)

    def step(after):
        try:
            steps.send(after)
        except StopIteration:
            pass

    def solve(level, value, ahead_of):
        top = bits[level]
        for bit in range(1, top):
            value = ahead_of.get(bit, lambda v: v)(value)
            value = value + across(value, bit)
        while level not in table:
            step(value)
        if top > 1:
            step(value)
            step(value)
        value = ahead_of.get(top, lambda v: v)(value)
        stacked = pair_up(low(top), value, across(value, top), 1)
        stacked = stacked / jnp.sqrt(jnp.float32(rows_here << top))
        return times_transposed(stacked, table[level])

    def update(corr, state, held):
        return state - jnp.einsum("ka,na->kn", held, corr, precision=HIGH)

    if leaf_core:
        top = pair_up(low(0), value, exchange(value, 1), 1)
        top = top / jnp.sqrt(jnp.float32(rows_here))
        held = times_transposed(top, table[first])
    else:
        held = chip_gather(solve(first, chip_sum(value), {}))
    state = update(corr_bases[first], state, held)
    value = chip_sum(project(proj_bases[first - 1], state))
    if heads:
        step(value)
        finish_table(heads[0][0], tie(fetched[0], value)[None])
    for level in reversed(range(1, first)):
        start = value
        held = solve(level, value, {})
        projs, corrs = lax.optimization_barrier((proj_bases, corr_bases, start))[:2]
        proj, corr = projs[level - 1], corrs[level]
        ahead = chip_sum(project(proj, state))
        own = jnp.einsum("na,nb->ab", proj, corr, precision=HIGH)
        if heads and level == first - 1:
            step(own)
        value = ahead - times_transposed(held, own + exchange(own, 1))
        if level > 1:
            state = update(corr, state, chip_gather(held))
    last_corrs = tie(corr_bases, value)
    one_corr, zero_corr = last_corrs[1], last_corrs[0]
    state = update(one_corr, state, chip_gather(held))
    ahead_of = {
        bits[0] - 1: lambda v: tie(v, zero_corr),
        bits[0]: lambda v: tie(v, state),
    }
    held = solve(0, value, ahead_of)
    return finish(state, zero_corr, chip_gather(held))


def solution(mesh):
    return jax.shard_map(
        on_device,
        mesh=mesh,
        in_specs=(
            P("leaf", None),
            P(None, "leaf", None),
            P(None, "leaf", None),
            P(None, "leaf", None),
        ),
        out_specs=P("leaf", None),
        check_vma=False,
    )
```

```python
import jax
import jax.numpy as jnp
from jax import lax
from jax.experimental import pallas as pl
from jax.experimental.pallas import tpu as pltpu
from jax.sharding import PartitionSpec as P

LEVELS = 5
HIGH = lax.Precision.HIGH
IN_HBM = pl.BlockSpec(memory_space=pltpu.HBM)
IN_VMEM = pl.BlockSpec(memory_space=pltpu.VMEM)


def exchange(value, mask):
    pairs = [(source, source ^ mask) for source in range(lax.axis_size("leaf"))]
    return lax.ppermute(value, "leaf", pairs)


def tie(value, after):
    return lax.optimization_barrier((value, after))[0]


def pair_up(low, mine, other, axis):
    return jnp.where(
        low,
        jnp.concatenate([mine, other], axis),
        jnp.concatenate([other, mine], axis),
    )


def project(basis, state):
    return jnp.einsum("kn,nr->kr", state, basis, precision=HIGH)


def times_transposed(left, right):
    return jnp.einsum("kb,ab->ka", left, right, precision=HIGH)


def parts(value):
    high = value.astype(jnp.bfloat16)
    return high, (value - high.astype(jnp.float32)).astype(jnp.bfloat16)


def three_passes(left, right, dim):
    rows = left.shape[0]
    left_high, left_low = parts(left)
    right_high, right_low = parts(right)

    def one(a, b):
        return lax.dot_general(a, b, (((1,), (dim,)), ((), ())), preferred_element_type=jnp.float32)

    both = one(jnp.concatenate([left_high, left_low], 0), right_high)
    return both[:rows] + (both[rows:] + one(left_high, right_low))


def begin(rhs, proj_bases, corr_bases, cores, first, leaf_core, groups):
    rows, width = rhs.shape
    rank = proj_bases.shape[2]
    shapes = [(width, rank), (width, rows)] + [(rows, rank)] * 4
    shapes += [(rank, 2 * rank)] if leaf_core else []
    shapes += [(sum(n for _, n in group), 2 * rank) for group in groups]

    def body(x_hbm, p_hbm, w_hbm, c_hbm, *refs):
        outs, (x_ref, p_ref, sems) = list(refs[: len(shapes)]), refs[len(shapes) :]
        q_out, state_out, w_out, p_out, w_next, p_next = outs[:6]
        rest = outs[6:]
        moves = [(x_hbm, x_ref), (p_hbm.at[first], p_ref)]
        if leaf_core:
            moves.append((c_hbm.at[first], rest.pop(0)))
        moves += [(w_hbm.at[first], w_out), (p_hbm.at[first - 1], p_out)]
        for group, out in zip(groups, rest):
            start = 0
            for level, n in group:
                moves.append((c_hbm.at[level, 0:n], out.at[start : start + n]))
                start += n
        moves += [(w_hbm.at[first - 1], w_next), (p_hbm.at[first - 2], p_next)]
        copies = [pltpu.make_async_copy(a, b, sems.at[at]) for at, (a, b) in enumerate(moves)]
        for copy in copies:
            copy.start()
        copies[0].wait()
        state = x_ref[...].T
        state_out[...] = state
        copies[1].wait()
        q_out[...] = three_passes(state, p_ref[...], 0)
        for copy in copies[2:]:
            copy.wait()

    count = 6 + (1 if leaf_core else 0) + sum(len(group) for group in groups)
    return pl.pallas_call(
        body,
        in_specs=[IN_HBM] * 4,
        out_specs=[IN_VMEM] * len(shapes),
        out_shape=[pltpu.VMEM(shape, jnp.float32) for shape in shapes],
        scratch_shapes=[
            pltpu.VMEM((rows, width), jnp.float32),
            pltpu.VMEM((rows, rank), jnp.float32),
            pltpu.SemaphoreType.DMA((count,)),
        ],
        compiler_params=pltpu.CompilerParams(vmem_limit_bytes=48 * 2**20),
        cost_estimate=pl.CostEstimate(
            flops=6 * rows * width * rank, bytes_accessed=2**22, transcendentals=0
        ),
        name="begin",
    )(rhs, proj_bases, corr_bases, cores)


def finish(state, corr, held):
    width, rows = state.shape

    def body(x_ref, w_ref, t_ref, out_ref):
        out_ref[...] = (x_ref[...] - three_passes(t_ref[...], w_ref[...], 1)).T

    return pl.pallas_call(
        body,
        in_specs=[IN_VMEM] * 3,
        out_specs=IN_VMEM,
        out_shape=jax.ShapeDtypeStruct((rows, width), jnp.float32),
        compiler_params=pltpu.CompilerParams(vmem_limit_bytes=16 * 2**20),
        cost_estimate=pl.CostEstimate(
            flops=6 * rows * width * corr.shape[1], bytes_accessed=2**21, transcendentals=0
        ),
        name="finish",
    )(state, corr, held)


def on_device(rhs, proj_bases, corr_bases, cores):
    count = lax.axis_size("leaf")
    me = lax.axis_index("leaf")
    rows_here, width = rhs.shape
    rank = proj_bases.shape[2]
    bits = [(count >> level).bit_length() - 2 for level in range(LEVELS)]
    first = LEVELS - 1
    chain = [level for level in reversed(range(LEVELS)) if bits[level] > 0]

    def low(bit):
        return (me >> bit) & 1 == 0

    parity = me & 1
    for bit in range(1, count.bit_length() - 1):
        parity = parity ^ ((me >> bit) & 1)
    upper = parity == 0

    def across(value, bit):
        return exchange(value, (1 << bit) | (1 if bit > 0 else 0))

    def chip_sum(value):
        half = width // 2
        keep = jnp.where(upper, value[:half], value[half:])
        send = jnp.where(upper, value[half:], value[:half])
        return keep + exchange(send, 1)

    def chip_gather(value):
        return pair_up(upper, value, exchange(value, 1), 0)

    heads = [(level, rank >> bits[level]) for level in chain if bits[level] == 1]
    tails = [(level, rank >> bits[level]) for level in chain if bits[level] > 1]
    groups = [group for group in (heads, tails) if group]
    leaf_core = bits[first] == 0
    value, state, top_corr, next_proj, next_corr, after_proj, *fetched = begin(
        rhs, proj_bases, corr_bases, cores, first, leaf_core, groups
    )

    table = {}
    if leaf_core:
        table[first] = fetched.pop(0)

    def finish_table(level, mine):
        part = exchange(mine, 1)
        both = jnp.where(low(0), jnp.stack([mine, part], 1), jnp.stack([part, mine], 1))
        table[level] = both.reshape(rank, 2 * rank)

    def gather_steps():
        block = fetched[-1][None]
        waiting = [level for level, _ in tails]
        bit = 1
        coming = exchange(block, 2)
        while True:
            after = yield
            block = pair_up(low(bit), block, tie(coming, after), 0)
            bit += 1
            after = yield
            rows = rank >> bit
            for level in [level for level in waiting if bits[level] == bit]:
                finish_table(level, tie(block[:, :rows], after))
                block = block[:, rows:]
            waiting = [level for level in waiting if bits[level] > bit]
            if waiting:
                coming = exchange(tie(block, after), 1 << bit)
            else:
                return

    steps = gather_steps()
    next(steps)

    def step(after):
        try:
            steps.send(after)
        except StopIteration:
            pass

    def solve(level, value, ahead_of):
        top = bits[level]
        for bit in range(1, top):
            value = ahead_of.get(bit, lambda v: v)(value)
            value = value + across(value, bit)
        while level not in table:
            step(value)
        if top > 1:
            step(value)
            step(value)
        value = ahead_of.get(top, lambda v: v)(value)
        stacked = pair_up(low(top), value, across(value, top), 1)
        stacked = stacked / jnp.sqrt(jnp.float32(rows_here << top))
        return times_transposed(stacked, table[level])

    def update(corr, state, held):
        return state - jnp.einsum("ka,na->kn", held, corr, precision=HIGH)

    if leaf_core:
        top = pair_up(low(0), value, exchange(value, 1), 1)
        top = top / jnp.sqrt(jnp.float32(rows_here))
        held = times_transposed(top, table[first])
    else:
        held = chip_gather(solve(first, chip_sum(value), {}))
    state = update(top_corr, state, held)
    value = chip_sum(project(next_proj, state))
    if heads:
        step(value)
        finish_table(heads[0][0], tie(fetched[0], value)[None])
    for level in reversed(range(1, first)):
        start = value
        held = solve(level, value, {})
        if level == first - 1:
            proj, corr = tie(after_proj, start), tie(next_corr, start)
        else:
            projs, corrs = lax.optimization_barrier((proj_bases, corr_bases, start))[:2]
            proj, corr = projs[level - 1], corrs[level]
        ahead = chip_sum(project(proj, state))
        own = jnp.einsum("na,nb->ab", proj, corr, precision=HIGH)
        if heads and level == first - 1:
            step(own)
        value = ahead - times_transposed(held, own + exchange(own, 1))
        if level > 1:
            state = update(corr, state, chip_gather(held))
    last_corrs = tie(corr_bases, value)
    one_corr, zero_corr = last_corrs[1], last_corrs[0]
    state = update(one_corr, state, chip_gather(held))
    ahead_of = {
        bits[0] - 1: lambda v: tie(v, zero_corr),
        bits[0]: lambda v: tie(v, state),
    }
    held = solve(0, value, ahead_of)
    return finish(state, zero_corr, chip_gather(held))


def solution(mesh):
    return jax.shard_map(
        on_device,
        mesh=mesh,
        in_specs=(
            P("leaf", None),
            P(None, "leaf", None),
            P(None, "leaf", None),
            P(None, "leaf", None),
        ),
        out_specs=P("leaf", None),
        check_vma=False,
    )
```

```python
import jax
import jax.numpy as jnp
from jax import lax
from jax.experimental import pallas as pl
from jax.experimental.pallas import tpu as pltpu
from jax.sharding import PartitionSpec as P

LEVELS = 5
HIGH = lax.Precision.HIGH
MIB = 2**20
IN_HBM = pl.BlockSpec(memory_space=pltpu.HBM)
IN_VMEM = pl.BlockSpec(memory_space=pltpu.VMEM)


def exchange(value, mask):
    pairs = [(source, source ^ mask) for source in range(lax.axis_size("leaf"))]
    return lax.ppermute(value, "leaf", pairs)


def tie(value, after):
    return lax.optimization_barrier((value, after))[0]


def pair_up(low, mine, other, axis):
    return jnp.where(
        low,
        jnp.concatenate([mine, other], axis),
        jnp.concatenate([other, mine], axis),
    )


def project(basis, state):
    return jnp.einsum("kn,nr->kr", state, basis, precision=HIGH)


def times_transposed(left, right):
    return jnp.einsum("kb,ab->ka", left, right, precision=HIGH)


def parts(value):
    high = value.astype(jnp.bfloat16)
    return high, (value - high.astype(jnp.float32)).astype(jnp.bfloat16)


def three_passes(left, right, dim):
    rows = left.shape[0]
    left_high, left_low = parts(left)
    right_high, right_low = parts(right)

    def one(a, b):
        return lax.dot_general(a, b, (((1,), (dim,)), ((), ())), preferred_element_type=jnp.float32)

    both = one(jnp.concatenate([left_high, left_low], 0), right_high)
    return both[:rows] + (both[rows:] + one(left_high, right_low))


def begin(rhs, proj_bases, corr_bases, cores, first, leaf_core, groups):
    rows, width = rhs.shape
    rank = proj_bases.shape[2]
    shapes = [(width, rank), (width, rows)] + [(rows, rank)] * 2
    shapes += [(rank, 2 * rank)] if leaf_core else []
    shapes += [(sum(n for _, n in group), 2 * rank) for group in groups]

    def body(x_hbm, p_hbm, w_hbm, c_hbm, *refs):
        outs, (x_ref, p_ref, sems) = list(refs[: len(shapes)]), refs[len(shapes) :]
        q_out, state_out, w_out, p_out = outs[:4]
        rest = outs[4:]
        moves = [(x_hbm, x_ref), (p_hbm.at[first], p_ref)]
        if leaf_core:
            moves.append((c_hbm.at[first], rest.pop(0)))
        moves += [(w_hbm.at[first], w_out), (p_hbm.at[first - 1], p_out)]
        for group, out in zip(groups, rest):
            start = 0
            for level, n in group:
                moves.append((c_hbm.at[level, 0:n], out.at[start : start + n]))
                start += n
        copies = [pltpu.make_async_copy(a, b, sems.at[at]) for at, (a, b) in enumerate(moves)]
        for copy in copies:
            copy.start()
        copies[0].wait()
        state = x_ref[...].T
        state_out[...] = state
        copies[1].wait()
        q_out[...] = three_passes(state, p_ref[...], 0)
        for copy in copies[2:]:
            copy.wait()

    count = 4 + (1 if leaf_core else 0) + sum(len(group) for group in groups)
    return pl.pallas_call(
        body,
        in_specs=[IN_HBM] * 4,
        out_specs=[IN_VMEM] * len(shapes),
        out_shape=[pltpu.VMEM(shape, jnp.float32) for shape in shapes],
        scratch_shapes=[
            pltpu.VMEM((rows, width), jnp.float32),
            pltpu.VMEM((rows, rank), jnp.float32),
            pltpu.SemaphoreType.DMA((count,)),
        ],
        compiler_params=pltpu.CompilerParams(vmem_limit_bytes=52 * MIB),
        cost_estimate=pl.CostEstimate(
            flops=6 * rows * width * rank, bytes_accessed=2**22, transcendentals=0
        ),
        name="begin",
    )(rhs, proj_bases, corr_bases, cores)


def fetch(proj_bases, corr_bases, projs, corrs, after):
    rows, rank = corr_bases.shape[1:]
    count = len(projs) + len(corrs)

    def body(p_hbm, w_hbm, _, *refs):
        sources = [p_hbm.at[level] for level in projs] + [w_hbm.at[level] for level in corrs]
        sems = refs[-1]
        copies = [
            pltpu.make_async_copy(source, out, sems.at[at])
            for at, (source, out) in enumerate(zip(sources, refs[:-1]))
        ]
        for copy in copies:
            copy.start()
        for copy in copies:
            copy.wait()

    return pl.pallas_call(
        body,
        in_specs=[IN_HBM, IN_HBM, pl.BlockSpec(memory_space=pl.ANY)],
        out_specs=[IN_VMEM] * count,
        out_shape=[pltpu.VMEM((rows, rank), jnp.float32)] * count,
        scratch_shapes=[pltpu.SemaphoreType.DMA((count,))],
        compiler_params=pltpu.CompilerParams(vmem_limit_bytes=(54 - count) * MIB),
        cost_estimate=pl.CostEstimate(
            flops=0, bytes_accessed=8 * count * rows * rank, transcendentals=0
        ),
        name="fetch",
    )(proj_bases, corr_bases, after)


def finish(state, corr, held):
    width, rows = state.shape

    def body(x_ref, w_ref, t_ref, out_ref):
        out_ref[...] = (x_ref[...] - three_passes(t_ref[...], w_ref[...], 1)).T

    return pl.pallas_call(
        body,
        in_specs=[IN_VMEM] * 3,
        out_specs=IN_VMEM,
        out_shape=jax.ShapeDtypeStruct((rows, width), jnp.float32),
        compiler_params=pltpu.CompilerParams(vmem_limit_bytes=16 * MIB),
        cost_estimate=pl.CostEstimate(
            flops=6 * rows * width * corr.shape[1], bytes_accessed=2**21, transcendentals=0
        ),
        name="finish",
    )(state, corr, held)


def on_device(rhs, proj_bases, corr_bases, cores):
    count = lax.axis_size("leaf")
    me = lax.axis_index("leaf")
    rows_here, width = rhs.shape
    rank = proj_bases.shape[2]
    bits = [(count >> level).bit_length() - 2 for level in range(LEVELS)]
    first = LEVELS - 1
    chain = [level for level in reversed(range(LEVELS)) if bits[level] > 0]

    def low(bit):
        return (me >> bit) & 1 == 0

    parity = me & 1
    for bit in range(1, count.bit_length() - 1):
        parity = parity ^ ((me >> bit) & 1)
    upper = parity == 0

    def across(value, bit):
        return exchange(value, (1 << bit) | (1 if bit > 0 else 0))

    def chip_sum(value):
        half = width // 2
        keep = jnp.where(upper, value[:half], value[half:])
        send = jnp.where(upper, value[half:], value[:half])
        return keep + exchange(send, 1)

    def chip_gather(value):
        return pair_up(upper, value, exchange(value, 1), 0)

    heads = [(level, rank >> bits[level]) for level in chain if bits[level] == 1]
    tails = [(level, rank >> bits[level]) for level in chain if bits[level] > 1]
    groups = [group for group in (heads, tails) if group]
    leaf_core = bits[first] == 0
    value, state, top_corr, next_proj, *fetched = begin(
        rhs, proj_bases, corr_bases, cores, first, leaf_core, groups
    )
    proj, corr = fetch(proj_bases, corr_bases, [first - 2], [first - 1], value)

    table = {}
    if leaf_core:
        table[first] = fetched.pop(0)

    def finish_table(level, mine):
        part = exchange(mine, 1)
        both = jnp.where(low(0), jnp.stack([mine, part], 1), jnp.stack([part, mine], 1))
        table[level] = both.reshape(rank, 2 * rank)

    def gather_steps():
        block = fetched[-1][None]
        waiting = [level for level, _ in tails]
        bit = 1
        coming = exchange(block, 2)
        while True:
            after = yield
            block = pair_up(low(bit), block, tie(coming, after), 0)
            bit += 1
            after = yield
            rows = rank >> bit
            for level in [level for level in waiting if bits[level] == bit]:
                finish_table(level, tie(block[:, :rows], after))
                block = block[:, rows:]
            waiting = [level for level in waiting if bits[level] > bit]
            if waiting:
                coming = exchange(tie(block, after), 1 << bit)
            else:
                return

    steps = gather_steps()
    next(steps)

    def step(after):
        try:
            steps.send(after)
        except StopIteration:
            pass

    def solve(level, value, ahead_of):
        top = bits[level]
        for bit in range(1, top):
            value = ahead_of.get(bit, lambda v: v)(value)
            value = value + across(value, bit)
        while level not in table:
            step(value)
        if top > 1:
            step(value)
            step(value)
        value = ahead_of.get(top, lambda v: v)(value)
        stacked = pair_up(low(top), value, across(value, top), 1)
        stacked = stacked / jnp.sqrt(jnp.float32(rows_here << top))
        return times_transposed(stacked, table[level])

    def update(corr, state, held):
        return state - jnp.einsum("ka,na->kn", held, corr, precision=HIGH)

    if leaf_core:
        top = pair_up(low(0), value, tie(exchange(value, 1), proj), 1)
        top = top / jnp.sqrt(jnp.float32(rows_here))
        held = times_transposed(top, table[first])
    else:
        held = chip_gather(solve(first, chip_sum(value), {}))
    state = update(top_corr, state, held)
    value = chip_sum(project(next_proj, state))
    if heads:
        step(value)
        finish_table(heads[0][0], tie(fetched[0], value)[None])
    for level in reversed(range(1, first)):
        start = value
        held = solve(level, value, {})
        if level == first - 2:
            later = fetch(
                proj_bases,
                corr_bases,
                list(reversed(range(level))),
                list(reversed(range(level + 1))),
                start,
            )
            projs, corrs = list(later[:level]), list(later[level:])
        if level < first - 1:
            proj, corr = projs.pop(0), corrs.pop(0)
        proj, corr = tie(proj, start), tie(corr, start)
        ahead = chip_sum(project(proj, state))
        own = jnp.einsum("na,nb->ab", proj, corr, precision=HIGH)
        if heads and level == first - 1:
            step(own)
        value = ahead - times_transposed(held, own + exchange(own, 1))
        if level > 1:
            state = update(corr, state, chip_gather(held))
    state = update(corr, state, chip_gather(held))
    ahead_of = {bits[0]: lambda v: tie(v, state)}
    held = solve(0, value, ahead_of)
    return finish(state, corrs[0], chip_gather(held))


def solution(mesh):
    return jax.shard_map(
        on_device,
        mesh=mesh,
        in_specs=(
            P("leaf", None),
            P(None, "leaf", None),
            P(None, "leaf", None),
            P(None, "leaf", None),
        ),
        out_specs=P("leaf", None),
        check_vma=False,
    )
```

```python
import jax
import jax.numpy as jnp
from jax import lax
from jax.experimental import pallas as pl
from jax.experimental.pallas import tpu as pltpu
from jax.sharding import PartitionSpec as P

LEVELS = 5
HIGH = lax.Precision.HIGH
MIB = 2**20
IN_HBM = pl.BlockSpec(memory_space=pltpu.HBM)
IN_VMEM = pl.BlockSpec(memory_space=pltpu.VMEM)


def exchange(value, mask):
    pairs = [(source, source ^ mask) for source in range(lax.axis_size("leaf"))]
    return lax.ppermute(value, "leaf", pairs)


def tie(value, after):
    return lax.optimization_barrier((value, after))[0]


def pair_up(low, mine, other, axis):
    return jnp.where(
        low,
        jnp.concatenate([mine, other], axis),
        jnp.concatenate([other, mine], axis),
    )


def project(basis, state):
    return jnp.einsum("kn,nr->kr", state, basis, precision=HIGH)


def times_transposed(left, right):
    return jnp.einsum("kb,ab->ka", left, right, precision=HIGH)


def parts(value):
    high = value.astype(jnp.bfloat16)
    return high, (value - high.astype(jnp.float32)).astype(jnp.bfloat16)


def three_passes(left, right, dim):
    rows = left.shape[0]
    left_high, left_low = parts(left)
    right_high, right_low = parts(right)

    def one(a, b):
        return lax.dot_general(a, b, (((1,), (dim,)), ((), ())), preferred_element_type=jnp.float32)

    both = one(jnp.concatenate([left_high, left_low], 0), right_high)
    return both[:rows] + (both[rows:] + one(left_high, right_low))


def begin(rhs, proj_bases, corr_bases, cores, first, leaf_core, groups):
    rows, width = rhs.shape
    rank = proj_bases.shape[2]
    shapes = [(width, rank), (width, rows)] + [(rows, rank)] * 4
    shapes += [(rank, 2 * rank)] if leaf_core else []
    shapes += [(sum(n for _, n in group), 2 * rank) for group in groups]

    def body(x_hbm, p_hbm, w_hbm, c_hbm, *refs):
        outs, (x_ref, p_ref, sems) = list(refs[: len(shapes)]), refs[len(shapes) :]
        q_out, state_out, w_out, p_out, w_next, p_next = outs[:6]
        rest = outs[6:]
        moves = [(x_hbm, x_ref), (p_hbm.at[first], p_ref)]
        if leaf_core:
            moves.append((c_hbm.at[first], rest.pop(0)))
        moves += [(w_hbm.at[first], w_out), (p_hbm.at[first - 1], p_out)]
        for group, out in zip(groups, rest):
            start = 0
            for level, n in group:
                moves.append((c_hbm.at[level, 0:n], out.at[start : start + n]))
                start += n
        moves += [(w_hbm.at[first - 1], w_next), (p_hbm.at[first - 2], p_next)]
        copies = [pltpu.make_async_copy(a, b, sems.at[at]) for at, (a, b) in enumerate(moves)]
        for copy in copies:
            copy.start()
        copies[0].wait()
        state = x_ref[...].T
        state_out[...] = state
        copies[1].wait()
        q_out[...] = three_passes(state, p_ref[...], 0)
        for copy in copies[2:]:
            copy.wait()

    count = 6 + (1 if leaf_core else 0) + sum(len(group) for group in groups)
    return pl.pallas_call(
        body,
        in_specs=[IN_HBM] * 4,
        out_specs=[IN_VMEM] * len(shapes),
        out_shape=[pltpu.VMEM(shape, jnp.float32) for shape in shapes],
        scratch_shapes=[
            pltpu.VMEM((rows, width), jnp.float32),
            pltpu.VMEM((rows, rank), jnp.float32),
            pltpu.SemaphoreType.DMA((count,)),
        ],
        compiler_params=pltpu.CompilerParams(vmem_limit_bytes=49 * MIB),
        cost_estimate=pl.CostEstimate(
            flops=6 * rows * width * rank, bytes_accessed=2**22, transcendentals=0
        ),
        name="begin",
    )(rhs, proj_bases, corr_bases, cores)


def fetch(proj_bases, corr_bases, projs, corrs, after):
    rows, rank = corr_bases.shape[1:]
    count = len(projs) + len(corrs)

    def body(p_hbm, w_hbm, _, *refs):
        sources = [p_hbm.at[level] for level in projs] + [w_hbm.at[level] for level in corrs]
        sems = refs[-1]
        copies = [
            pltpu.make_async_copy(source, out, sems.at[at])
            for at, (source, out) in enumerate(zip(sources, refs[:-1]))
        ]
        for copy in copies:
            copy.start()
        for copy in copies:
            copy.wait()

    return pl.pallas_call(
        body,
        in_specs=[IN_HBM, IN_HBM, pl.BlockSpec(memory_space=pl.ANY)],
        out_specs=[IN_VMEM] * count,
        out_shape=[pltpu.VMEM((rows, rank), jnp.float32)] * count,
        scratch_shapes=[pltpu.SemaphoreType.DMA((count,))],
        compiler_params=pltpu.CompilerParams(vmem_limit_bytes=45 * MIB),
        cost_estimate=pl.CostEstimate(
            flops=0, bytes_accessed=8 * count * rows * rank, transcendentals=0
        ),
        name="fetch",
    )(proj_bases, corr_bases, after)


def finish(state, corr, held):
    width, rows = state.shape

    def body(x_ref, w_ref, t_ref, out_ref):
        out_ref[...] = (x_ref[...] - three_passes(t_ref[...], w_ref[...], 1)).T

    return pl.pallas_call(
        body,
        in_specs=[IN_VMEM] * 3,
        out_specs=IN_VMEM,
        out_shape=jax.ShapeDtypeStruct((rows, width), jnp.float32),
        compiler_params=pltpu.CompilerParams(vmem_limit_bytes=16 * MIB),
        cost_estimate=pl.CostEstimate(
            flops=6 * rows * width * corr.shape[1], bytes_accessed=2**21, transcendentals=0
        ),
        name="finish",
    )(state, corr, held)


def on_device(rhs, proj_bases, corr_bases, cores):
    count = lax.axis_size("leaf")
    me = lax.axis_index("leaf")
    rows_here, width = rhs.shape
    rank = proj_bases.shape[2]
    bits = [(count >> level).bit_length() - 2 for level in range(LEVELS)]
    first = LEVELS - 1
    chain = [level for level in reversed(range(LEVELS)) if bits[level] > 0]

    def low(bit):
        return (me >> bit) & 1 == 0

    parity = me & 1
    for bit in range(1, count.bit_length() - 1):
        parity = parity ^ ((me >> bit) & 1)
    upper = parity == 0

    def across(value, bit):
        return exchange(value, (1 << bit) | (1 if bit > 0 else 0))

    def chip_sum(value):
        half = width // 2
        keep = jnp.where(upper, value[:half], value[half:])
        send = jnp.where(upper, value[half:], value[:half])
        return keep + exchange(send, 1)

    def chip_gather(value):
        return pair_up(upper, value, exchange(value, 1), 0)

    heads = [(level, rank >> bits[level]) for level in chain if bits[level] == 1]
    tails = [(level, rank >> bits[level]) for level in chain if bits[level] > 1]
    groups = [group for group in (heads, tails) if group]
    leaf_core = bits[first] == 0
    value, state, top_corr, next_proj, corr, proj, *fetched = begin(
        rhs, proj_bases, corr_bases, cores, first, leaf_core, groups
    )

    table = {}
    if leaf_core:
        table[first] = fetched.pop(0)

    def finish_table(level, mine):
        part = exchange(mine, 1)
        both = jnp.where(low(0), jnp.stack([mine, part], 1), jnp.stack([part, mine], 1))
        table[level] = both.reshape(rank, 2 * rank)

    def gather_steps():
        block = fetched[-1][None]
        waiting = [level for level, _ in tails]
        bit = 1
        coming = exchange(block, 2)
        while True:
            after = yield
            block = pair_up(low(bit), block, tie(coming, after), 0)
            bit += 1
            after = yield
            rows = rank >> bit
            for level in [level for level in waiting if bits[level] == bit]:
                finish_table(level, tie(block[:, :rows], after))
                block = block[:, rows:]
            waiting = [level for level in waiting if bits[level] > bit]
            if waiting:
                coming = exchange(tie(block, after), 1 << bit)
            else:
                return

    steps = gather_steps()
    next(steps)

    def step(after):
        try:
            steps.send(after)
        except StopIteration:
            pass

    def solve(level, value, ahead_of):
        top = bits[level]
        for bit in range(1, top):
            value = ahead_of.get(bit, lambda v: v)(value)
            value = value + across(value, bit)
        while level not in table:
            step(value)
        if level == 1:
            step(value)
            step(value)
        value = ahead_of.get(top, lambda v: v)(value)
        stacked = pair_up(low(top), value, across(value, top), 1)
        stacked = stacked / jnp.sqrt(jnp.float32(rows_here << top))
        return times_transposed(stacked, table[level])

    def update(corr, state, held):
        return state - jnp.einsum("ka,na->kn", held, corr, precision=HIGH)

    if leaf_core:
        top = pair_up(low(0), value, exchange(value, 1), 1)
        top = top / jnp.sqrt(jnp.float32(rows_here))
        held = times_transposed(top, table[first])
    else:
        held = chip_gather(solve(first, chip_sum(value), {}))
    state = update(top_corr, state, held)
    value = chip_sum(project(next_proj, state))
    if heads:
        finish_table(heads[0][0], tie(fetched[0], value)[None])
    for level in reversed(range(1, first)):
        start = value
        if heads and level < first - 1:
            step(start)
            step(start)
        held = solve(level, value, {})
        if level == first - 2:
            later = fetch(
                proj_bases,
                corr_bases,
                list(reversed(range(level))),
                list(reversed(range(level + 1))),
                start,
            )
            projs, corrs = list(later[:level]), list(later[level:])
        if level < first - 1:
            proj, corr = projs.pop(0), corrs.pop(0)
        proj, corr = tie(proj, start), tie(corr, start)
        ahead = chip_sum(project(proj, state))
        own = jnp.einsum("na,nb->ab", proj, corr, precision=HIGH)
        value = ahead - times_transposed(held, own + exchange(own, 1))
        if level > 1:
            state = update(corr, state, chip_gather(held))
    state = update(corr, state, chip_gather(held))
    ahead_of = {bits[0]: lambda v: tie(v, state)}
    held = solve(0, value, ahead_of)
    return finish(state, corrs[0], chip_gather(held))


def solution(mesh):
    return jax.shard_map(
        on_device,
        mesh=mesh,
        in_specs=(
            P("leaf", None),
            P(None, "leaf", None),
            P(None, "leaf", None),
            P(None, "leaf", None),
        ),
        out_specs=P("leaf", None),
        check_vma=False,
    )
```

```python
import jax
import jax.numpy as jnp
from jax import lax
from jax.experimental import pallas as pl
from jax.experimental.pallas import tpu as pltpu
from jax.sharding import PartitionSpec as P

LEVELS = 5
HIGH = lax.Precision.HIGH
MIB = 2**20
IN_HBM = pl.BlockSpec(memory_space=pltpu.HBM)
IN_VMEM = pl.BlockSpec(memory_space=pltpu.VMEM)


def exchange(value, mask):
    pairs = [(source, source ^ mask) for source in range(lax.axis_size("leaf"))]
    return lax.ppermute(value, "leaf", pairs)


def tie(value, after):
    return lax.optimization_barrier((value, after))[0]


def pair_up(low, mine, other, axis):
    return jnp.where(
        low,
        jnp.concatenate([mine, other], axis),
        jnp.concatenate([other, mine], axis),
    )


def project(basis, state):
    return jnp.einsum("kn,nr->kr", state, basis, precision=HIGH)


def times_transposed(left, right):
    return jnp.einsum("kb,ab->ka", left, right, precision=HIGH)


def parts(value):
    high = value.astype(jnp.bfloat16)
    return high, (value - high.astype(jnp.float32)).astype(jnp.bfloat16)


def three_passes(left, right, dim):
    rows = left.shape[0]
    left_high, left_low = parts(left)
    right_high, right_low = parts(right)

    def one(a, b):
        return lax.dot_general(a, b, (((1,), (dim,)), ((), ())), preferred_element_type=jnp.float32)

    both = one(jnp.concatenate([left_high, left_low], 0), right_high)
    return both[:rows] + (both[rows:] + one(left_high, right_low))


def begin(rhs, proj_bases, corr_bases, cores, first, leaf_core, groups):
    rows, width = rhs.shape
    rank = proj_bases.shape[2]
    shapes = [(width, rank), (width, rows)] + [(rows, rank)] * 4
    shapes += [(rank, 2 * rank)] if leaf_core else []
    shapes += [(sum(n for _, n in group), 2 * rank) for group in groups]

    def body(x_hbm, p_hbm, w_hbm, c_hbm, *refs):
        outs, (x_ref, p_ref, sems) = list(refs[: len(shapes)]), refs[len(shapes) :]
        q_out, state_out, w_out, p_out, w_next, p_next = outs[:6]
        rest = outs[6:]
        moves = [(x_hbm, x_ref), (p_hbm.at[first], p_ref)]
        if leaf_core:
            moves.append((c_hbm.at[first], rest.pop(0)))
        moves += [(w_hbm.at[first], w_out), (p_hbm.at[first - 1], p_out)]
        for group, out in zip(groups, rest):
            start = 0
            for level, n in group:
                moves.append((c_hbm.at[level, 0:n], out.at[start : start + n]))
                start += n
        moves += [(w_hbm.at[first - 1], w_next), (p_hbm.at[first - 2], p_next)]
        copies = [pltpu.make_async_copy(a, b, sems.at[at]) for at, (a, b) in enumerate(moves)]
        for copy in copies:
            copy.start()
        copies[0].wait()
        state = x_ref[...].T
        state_out[...] = state
        copies[1].wait()
        q_out[...] = three_passes(state, p_ref[...], 0)
        for copy in copies[2:]:
            copy.wait()

    count = 6 + (1 if leaf_core else 0) + sum(len(group) for group in groups)
    return pl.pallas_call(
        body,
        in_specs=[IN_HBM] * 4,
        out_specs=[IN_VMEM] * len(shapes),
        out_shape=[pltpu.VMEM(shape, jnp.float32) for shape in shapes],
        scratch_shapes=[
            pltpu.VMEM((rows, width), jnp.float32),
            pltpu.VMEM((rows, rank), jnp.float32),
            pltpu.SemaphoreType.DMA((count,)),
        ],
        compiler_params=pltpu.CompilerParams(vmem_limit_bytes=49 * MIB),
        cost_estimate=pl.CostEstimate(
            flops=6 * rows * width * rank, bytes_accessed=2**22, transcendentals=0
        ),
        name="begin",
    )(rhs, proj_bases, corr_bases, cores)


def fetch(proj_bases, corr_bases, projs, corrs, after):
    rows, rank = corr_bases.shape[1:]
    count = len(projs) + len(corrs)

    def body(p_hbm, w_hbm, _, *refs):
        sources = [p_hbm.at[level] for level in projs] + [w_hbm.at[level] for level in corrs]
        sems = refs[-1]
        copies = [
            pltpu.make_async_copy(source, out, sems.at[at])
            for at, (source, out) in enumerate(zip(sources, refs[:-1]))
        ]
        for copy in copies:
            copy.start()
        for copy in copies:
            copy.wait()

    return pl.pallas_call(
        body,
        in_specs=[IN_HBM, IN_HBM, pl.BlockSpec(memory_space=pl.ANY)],
        out_specs=[IN_VMEM] * count,
        out_shape=[pltpu.VMEM((rows, rank), jnp.float32)] * count,
        scratch_shapes=[pltpu.SemaphoreType.DMA((count,))],
        compiler_params=pltpu.CompilerParams(vmem_limit_bytes=45 * MIB),
        cost_estimate=pl.CostEstimate(
            flops=0, bytes_accessed=8 * count * rows * rank, transcendentals=0
        ),
        name="fetch",
    )(proj_bases, corr_bases, after)


def finish(state, corr, held):
    width, rows = state.shape

    def body(x_ref, w_ref, t_ref, out_ref):
        out_ref[...] = (x_ref[...] - three_passes(t_ref[...], w_ref[...], 1)).T

    return pl.pallas_call(
        body,
        in_specs=[IN_VMEM] * 3,
        out_specs=IN_VMEM,
        out_shape=jax.ShapeDtypeStruct((rows, width), jnp.float32),
        compiler_params=pltpu.CompilerParams(vmem_limit_bytes=16 * MIB),
        cost_estimate=pl.CostEstimate(
            flops=6 * rows * width * corr.shape[1], bytes_accessed=2**21, transcendentals=0
        ),
        name="finish",
    )(state, corr, held)


def on_device(rhs, proj_bases, corr_bases, cores):
    count = lax.axis_size("leaf")
    me = lax.axis_index("leaf")
    rows_here, width = rhs.shape
    rank = proj_bases.shape[2]
    bits = [(count >> level).bit_length() - 2 for level in range(LEVELS)]
    first = LEVELS - 1
    chain = [level for level in reversed(range(LEVELS)) if bits[level] > 0]

    parity = me & 1
    for bit in range(1, count.bit_length() - 1):
        parity = parity ^ ((me >> bit) & 1)
    lows = [(me >> bit) & 1 == 0 for bit in range(count.bit_length() - 1)]
    rhs, upper, *lows = lax.optimization_barrier((rhs, parity == 0, *lows))

    def low(bit):
        return lows[bit]

    def across(value, bit):
        return exchange(value, (1 << bit) | (1 if bit > 0 else 0))

    def chip_sum(value):
        half = width // 2
        keep = jnp.where(upper, value[:half], value[half:])
        send = jnp.where(upper, value[half:], value[:half])
        return keep + exchange(send, 1)

    def chip_gather(value):
        return pair_up(upper, value, exchange(value, 1), 0)

    heads = [(level, rank >> bits[level]) for level in chain if bits[level] == 1]
    tails = [(level, rank >> bits[level]) for level in chain if bits[level] > 1]
    groups = [group for group in (heads, tails) if group]
    leaf_core = bits[first] == 0
    value, state, top_corr, next_proj, corr, proj, *fetched = begin(
        rhs, proj_bases, corr_bases, cores, first, leaf_core, groups
    )

    table = {}
    if leaf_core:
        table[first] = fetched.pop(0)

    def finish_table(level, mine):
        part = exchange(mine, 1)
        both = jnp.where(low(0), jnp.stack([mine, part], 1), jnp.stack([part, mine], 1))
        table[level] = both.reshape(rank, 2 * rank)

    def gather_steps():
        block = fetched[-1][None]
        waiting = [level for level, _ in tails]
        bit = 1
        coming = exchange(block, 2)
        while True:
            after = yield
            block = pair_up(low(bit), block, tie(coming, after), 0)
            bit += 1
            after = yield
            rows = rank >> bit
            for level in [level for level in waiting if bits[level] == bit]:
                finish_table(level, tie(block[:, :rows], after))
                block = block[:, rows:]
            waiting = [level for level in waiting if bits[level] > bit]
            if waiting:
                coming = exchange(tie(block, after), 1 << bit)
            else:
                return

    steps = gather_steps()
    next(steps)

    def step(after):
        try:
            steps.send(after)
        except StopIteration:
            pass

    def solve(level, value, ahead_of):
        top = bits[level]
        for bit in range(1, top):
            value = ahead_of.get(bit, lambda v: v)(value)
            value = value + across(value, bit)
        while level not in table:
            step(value)
        if level == 1:
            step(value)
            step(value)
        value = ahead_of.get(top, lambda v: v)(value)
        stacked = pair_up(low(top), value, across(value, top), 1)
        stacked = stacked / jnp.sqrt(jnp.float32(rows_here << top))
        return times_transposed(stacked, table[level])

    def update(corr, state, held):
        return state - jnp.einsum("ka,na->kn", held, corr, precision=HIGH)

    if leaf_core:
        top = pair_up(low(0), value, exchange(value, 1), 1)
        top = top / jnp.sqrt(jnp.float32(rows_here))
        held = times_transposed(top, table[first])
    else:
        held = chip_gather(solve(first, chip_sum(value), {}))
    state = update(top_corr, state, held)
    value = chip_sum(project(next_proj, state))
    if heads:
        finish_table(heads[0][0], tie(fetched[0], value)[None])
    for level in reversed(range(1, first)):
        start = value
        if heads and level < first - 1:
            step(start)
            step(start)
        held = solve(level, value, {})
        if level == first - 2:
            later = fetch(
                proj_bases,
                corr_bases,
                list(reversed(range(level))),
                list(reversed(range(level + 1))),
                start,
            )
            projs, corrs = list(later[:level]), list(later[level:])
        if level < first - 1:
            proj, corr = projs.pop(0), corrs.pop(0)
        proj, corr = tie(proj, start), tie(corr, start)
        ahead = chip_sum(project(proj, state))
        own = jnp.einsum("na,nb->ab", proj, corr, precision=HIGH)
        value = ahead - times_transposed(held, own + exchange(own, 1))
        if level > 1:
            state = update(corr, state, chip_gather(held))
    state = update(corr, state, chip_gather(held))
    ahead_of = {bits[0]: lambda v: tie(v, state)}
    held = solve(0, value, ahead_of)
    return finish(state, corrs[0], chip_gather(held))


def solution(mesh):
    return jax.shard_map(
        on_device,
        mesh=mesh,
        in_specs=(
            P("leaf", None),
            P(None, "leaf", None),
            P(None, "leaf", None),
            P(None, "leaf", None),
        ),
        out_specs=P("leaf", None),
        check_vma=False,
    )
```

```python
import jax
import jax.numpy as jnp
from jax import lax
from jax.experimental import pallas as pl
from jax.experimental.pallas import tpu as pltpu
from jax.sharding import PartitionSpec as P

LEVELS = 5
HIGH = lax.Precision.HIGH
MIB = 2**20
IN_HBM = pl.BlockSpec(memory_space=pltpu.HBM)
IN_VMEM = pl.BlockSpec(memory_space=pltpu.VMEM)


def exchange(value, mask):
    pairs = [(source, source ^ mask) for source in range(lax.axis_size("leaf"))]
    return lax.ppermute(value, "leaf", pairs)


def tie(value, after):
    return lax.optimization_barrier((value, after))[0]


def pair_up(low, mine, other, axis):
    return jnp.where(
        low,
        jnp.concatenate([mine, other], axis),
        jnp.concatenate([other, mine], axis),
    )


def project(basis, state):
    return jnp.einsum("kn,nr->kr", state, basis, precision=HIGH)


def times_transposed(left, right):
    return jnp.einsum("kb,ab->ka", left, right, precision=HIGH)


def parts(value):
    high = value.astype(jnp.bfloat16)
    return high, (value - high.astype(jnp.float32)).astype(jnp.bfloat16)


def three_passes(left, right, dim):
    rows = left.shape[0]
    left_high, left_low = parts(left)
    right_high, right_low = parts(right)

    def one(a, b):
        return lax.dot_general(a, b, (((1,), (dim,)), ((), ())), preferred_element_type=jnp.float32)

    both = one(jnp.concatenate([left_high, left_low], 0), right_high)
    return both[:rows] + (both[rows:] + one(left_high, right_low))


def begin(rhs, proj_bases, corr_bases, cores, first, leaf_core, groups):
    rows, width = rhs.shape
    rank = proj_bases.shape[2]
    shapes = [(width, rank), (width, rows)] + [(rows, rank)] * 4
    shapes += [(rank, 2 * rank)] if leaf_core else []
    shapes += [(sum(n for _, n in group), 2 * rank) for group in groups]

    def body(x_hbm, p_hbm, w_hbm, c_hbm, *refs):
        outs, (x_ref, p_ref, sems) = list(refs[: len(shapes)]), refs[len(shapes) :]
        q_out, state_out, w_out, p_out, w_next, p_next = outs[:6]
        rest = outs[6:]
        moves = [(x_hbm, x_ref), (p_hbm.at[first], p_ref)]
        if leaf_core:
            moves.append((c_hbm.at[first], rest.pop(0)))
        moves += [(w_hbm.at[first], w_out), (p_hbm.at[first - 1], p_out)]
        for group, out in zip(groups, rest):
            start = 0
            for level, n in group:
                moves.append((c_hbm.at[level, 0:n], out.at[start : start + n]))
                start += n
        moves += [(w_hbm.at[first - 1], w_next), (p_hbm.at[first - 2], p_next)]
        copies = [pltpu.make_async_copy(a, b, sems.at[at]) for at, (a, b) in enumerate(moves)]
        for copy in copies:
            copy.start()
        copies[0].wait()
        state = x_ref[...].T
        state_out[...] = state
        copies[1].wait()
        q_out[...] = three_passes(state, p_ref[...], 0)
        for copy in copies[2:]:
            copy.wait()

    count = 6 + (1 if leaf_core else 0) + sum(len(group) for group in groups)
    return pl.pallas_call(
        body,
        in_specs=[IN_HBM] * 4,
        out_specs=[IN_VMEM] * len(shapes),
        out_shape=[pltpu.VMEM(shape, jnp.float32) for shape in shapes],
        scratch_shapes=[
            pltpu.VMEM((rows, width), jnp.float32),
            pltpu.VMEM((rows, rank), jnp.float32),
            pltpu.SemaphoreType.DMA((count,)),
        ],
        compiler_params=pltpu.CompilerParams(vmem_limit_bytes=49 * MIB),
        cost_estimate=pl.CostEstimate(
            flops=6 * rows * width * rank, bytes_accessed=2**22, transcendentals=0
        ),
        name="begin",
    )(rhs, proj_bases, corr_bases, cores)


def fetch(proj_bases, corr_bases, projs, corrs, after):
    rows, rank = corr_bases.shape[1:]
    count = len(projs) + len(corrs)

    def body(p_hbm, w_hbm, _, *refs):
        sources = [p_hbm.at[level] for level in projs] + [w_hbm.at[level] for level in corrs]
        sems = refs[-1]
        copies = [
            pltpu.make_async_copy(source, out, sems.at[at])
            for at, (source, out) in enumerate(zip(sources, refs[:-1]))
        ]
        for copy in copies:
            copy.start()
        for copy in copies:
            copy.wait()

    return pl.pallas_call(
        body,
        in_specs=[IN_HBM, IN_HBM, pl.BlockSpec(memory_space=pl.ANY)],
        out_specs=[IN_VMEM] * count,
        out_shape=[pltpu.VMEM((rows, rank), jnp.float32)] * count,
        scratch_shapes=[pltpu.SemaphoreType.DMA((count,))],
        compiler_params=pltpu.CompilerParams(vmem_limit_bytes=50 * MIB),
        cost_estimate=pl.CostEstimate(
            flops=0, bytes_accessed=2**16, transcendentals=0
        ),
        name="fetch",
    )(proj_bases, corr_bases, after)


def finish(state, corr, held):
    width, rows = state.shape

    def body(x_ref, w_ref, t_ref, out_ref):
        out_ref[...] = (x_ref[...] - three_passes(t_ref[...], w_ref[...], 1)).T

    return pl.pallas_call(
        body,
        in_specs=[IN_VMEM] * 3,
        out_specs=IN_VMEM,
        out_shape=jax.ShapeDtypeStruct((rows, width), jnp.float32),
        compiler_params=pltpu.CompilerParams(vmem_limit_bytes=16 * MIB),
        cost_estimate=pl.CostEstimate(
            flops=6 * rows * width * corr.shape[1], bytes_accessed=2**21, transcendentals=0
        ),
        name="finish",
    )(state, corr, held)


def on_device(rhs, proj_bases, corr_bases, cores):
    count = lax.axis_size("leaf")
    me = lax.axis_index("leaf")
    rows_here, width = rhs.shape
    rank = proj_bases.shape[2]
    bits = [(count >> level).bit_length() - 2 for level in range(LEVELS)]
    first = LEVELS - 1
    chain = [level for level in reversed(range(LEVELS)) if bits[level] > 0]

    parity = me & 1
    for bit in range(1, count.bit_length() - 1):
        parity = parity ^ ((me >> bit) & 1)
    lows = [(me >> bit) & 1 == 0 for bit in range(count.bit_length() - 1)]
    rhs, upper, *lows = lax.optimization_barrier((rhs, parity == 0, *lows))

    def low(bit):
        return lows[bit]

    def across(value, bit):
        return exchange(value, (1 << bit) | (1 if bit > 0 else 0))

    def chip_sum(value):
        half = width // 2
        keep = jnp.where(upper, value[:half], value[half:])
        send = jnp.where(upper, value[half:], value[:half])
        return keep + exchange(send, 1)

    def chip_gather(value):
        return pair_up(upper, value, exchange(value, 1), 0)

    heads = [(level, rank >> bits[level]) for level in chain if bits[level] == 1]
    tails = [(level, rank >> bits[level]) for level in chain if bits[level] > 1]
    near = [item for item in tails if heads and bits[item[0]] == 2]
    far = [item for item in tails if item not in near]
    groups = [group for group in (heads, near, far) if group]
    leaf_core = bits[first] == 0
    value, state, top_corr, next_proj, corr, proj, *fetched = begin(
        rhs, proj_bases, corr_bases, cores, first, leaf_core, groups
    )

    table = {}
    if leaf_core:
        table[first] = fetched.pop(0)

    def finish_table(level, mine):
        part = exchange(mine, 1)
        both = jnp.where(low(0), jnp.stack([mine, part], 1), jnp.stack([part, mine], 1))
        table[level] = both.reshape(rank, 2 * rank)

    def gather_steps(items, block, after):
        waiting = [level for level, _ in items]
        bit = 1
        coming = exchange(block if after is None else tie(block, after), 2)
        while True:
            after = yield
            block = pair_up(low(bit), block, tie(coming, after), 0)
            bit += 1
            after = yield
            rows = rank >> bit
            for level in [level for level in waiting if bits[level] == bit]:
                finish_table(level, tie(block[:, :rows], after))
                block = block[:, rows:]
            waiting = [level for level in waiting if bits[level] > bit]
            if not waiting:
                return
            after = yield
            coming = exchange(tie(block, after), 1 << bit)

    gathers = []

    def open_gather(items, block, after):
        steps = gather_steps(items, block[None], after)
        next(steps)
        gathers.append(steps)

    def step(after):
        try:
            gathers[0].send(after)
        except StopIteration:
            gathers.pop(0)

    if near:
        open_gather(near, fetched[1], None)
    else:
        open_gather(far, fetched[-1], None)

    def solve(level, value, ahead_of, later=None, fetch_rest=None):
        top = bits[level]
        for bit in range(1, top):
            value = ahead_of.get(bit, lambda v: v)(value)
            value = value + across(value, bit)
        if near and level == near[0][0]:
            open_gather(far, fetched[2], value)
        while level not in table:
            step(value)
        if fetch_rest is not None:
            later.append(fetch_rest(value))
        value = ahead_of.get(top, lambda v: v)(value)
        stacked = pair_up(low(top), value, across(value, top), 1)
        stacked = stacked / jnp.sqrt(jnp.float32(rows_here << top))
        return times_transposed(stacked, table[level])

    def update(corr, state, held):
        return state - jnp.einsum("ka,na->kn", held, corr, precision=HIGH)

    if leaf_core:
        top = pair_up(low(0), value, exchange(value, 1), 1)
        top = top / jnp.sqrt(jnp.float32(rows_here))
        held = times_transposed(top, table[first])
    else:
        held = chip_gather(solve(first, chip_sum(value), {}))
    state = update(top_corr, state, held)
    value = chip_sum(project(next_proj, state))
    if heads:
        finish_table(heads[0][0], tie(fetched[0], value)[None])
    later = []
    for level in reversed(range(1, first)):
        start = value
        if near and level == near[0][0]:
            step(start)
            step(start)
        elif near and level < near[0][0]:
            for _ in range(3):
                step(start)
        if level == first - 1:
            later.append(fetch(proj_bases, corr_bases, [level - 2], [level - 1], start))
        if level == first - 2:
            fetch_rest = lambda v: fetch(
                proj_bases, corr_bases, list(reversed(range(level - 1))), list(reversed(range(level))), v
            )
        held = solve(level, value, {}, later, fetch_rest if level == first - 2 else None)
        if level < first - 1:
            proj, corr = (later[0][0], later[0][1]) if level == first - 2 else (later[1][0], later[1][1])
        proj, corr = tie(proj, start), tie(corr, start)
        ahead = chip_sum(project(proj, state))
        own = jnp.einsum("na,nb->ab", proj, corr, precision=HIGH)
        value = ahead - times_transposed(held, own + exchange(own, 1))
        if level > 1:
            state = update(corr, state, chip_gather(held))
    gathered = chip_gather(held)
    state = update(corr, state, gathered)
    ahead_of = {bits[0] - 1: lambda v: tie(v, gathered)}
    if near:
        step(value)
    held = solve(0, value, ahead_of)
    return finish(state, later[1][2], chip_gather(held))


def solution(mesh):
    return jax.shard_map(
        on_device,
        mesh=mesh,
        in_specs=(
            P("leaf", None),
            P(None, "leaf", None),
            P(None, "leaf", None),
            P(None, "leaf", None),
        ),
        out_specs=P("leaf", None),
        check_vma=False,
    )
```

```python
import jax
import jax.numpy as jnp
from jax import lax
from jax.experimental import pallas as pl
from jax.experimental.pallas import tpu as pltpu
from jax.sharding import PartitionSpec as P

LEVELS = 5
HIGH = lax.Precision.HIGH
MIB = 2**20
IN_HBM = pl.BlockSpec(memory_space=pltpu.HBM)
IN_VMEM = pl.BlockSpec(memory_space=pltpu.VMEM)


def exchange(value, mask):
    pairs = [(source, source ^ mask) for source in range(lax.axis_size("leaf"))]
    return lax.ppermute(value, "leaf", pairs)


def tie(value, after):
    return lax.optimization_barrier((value, after))[0]


def pair_up(low, mine, other, axis):
    return jnp.where(
        low,
        jnp.concatenate([mine, other], axis),
        jnp.concatenate([other, mine], axis),
    )


def project(basis, state):
    return jnp.einsum("kn,nr->kr", state, basis, precision=HIGH)


def times_transposed(left, right):
    return jnp.einsum("kb,ab->ka", left, right, precision=HIGH)


def parts(value):
    high = value.astype(jnp.bfloat16)
    return high, (value - high.astype(jnp.float32)).astype(jnp.bfloat16)


def three_passes(left, right, dim):
    rows = left.shape[0]
    left_high, left_low = parts(left)
    right_high, right_low = parts(right)

    def one(a, b):
        return lax.dot_general(a, b, (((1,), (dim,)), ((), ())), preferred_element_type=jnp.float32)

    both = one(jnp.concatenate([left_high, left_low], 0), right_high)
    return both[:rows] + (both[rows:] + one(left_high, right_low))


def begin(rhs, proj_bases, corr_bases, cores, first, leaf_core, groups):
    rows, width = rhs.shape
    rank = proj_bases.shape[2]
    shapes = [(width, rank), (width, rows)] + [(rows, rank)] * 4
    shapes += [(rank, 2 * rank)] if leaf_core else []
    shapes += [(sum(n for _, n in group), 2 * rank) for group in groups]

    def body(x_hbm, p_hbm, w_hbm, c_hbm, *refs):
        outs, (x_ref, p_ref, sems) = list(refs[: len(shapes)]), refs[len(shapes) :]
        q_out, state_out, w_out, p_out, w_next, p_next = outs[:6]
        rest = outs[6:]
        moves = [(x_hbm, x_ref), (p_hbm.at[first], p_ref)]
        if leaf_core:
            moves.append((c_hbm.at[first], rest.pop(0)))
        moves += [(w_hbm.at[first], w_out), (p_hbm.at[first - 1], p_out)]
        for group, out in zip(groups, rest):
            start = 0
            for level, n in group:
                moves.append((c_hbm.at[level, 0:n], out.at[start : start + n]))
                start += n
        moves += [(w_hbm.at[first - 1], w_next), (p_hbm.at[first - 2], p_next)]
        copies = [pltpu.make_async_copy(a, b, sems.at[at]) for at, (a, b) in enumerate(moves)]
        for copy in copies:
            copy.start()
        copies[0].wait()
        state = x_ref[...].T
        state_out[...] = state
        copies[1].wait()
        q_out[...] = three_passes(state, p_ref[...], 0)
        for copy in copies[2:]:
            copy.wait()

    count = 6 + (1 if leaf_core else 0) + sum(len(group) for group in groups)
    return pl.pallas_call(
        body,
        in_specs=[IN_HBM] * 4,
        out_specs=[IN_VMEM] * len(shapes),
        out_shape=[pltpu.VMEM(shape, jnp.float32) for shape in shapes],
        scratch_shapes=[
            pltpu.VMEM((rows, width), jnp.float32),
            pltpu.VMEM((rows, rank), jnp.float32),
            pltpu.SemaphoreType.DMA((count,)),
        ],
        compiler_params=pltpu.CompilerParams(vmem_limit_bytes=49 * MIB),
        cost_estimate=pl.CostEstimate(
            flops=6 * rows * width * rank, bytes_accessed=2**22, transcendentals=0
        ),
        name="begin",
    )(rhs, proj_bases, corr_bases, cores)


def fetch(proj_bases, corr_bases, projs, corrs, after):
    rows, rank = corr_bases.shape[1:]
    count = len(projs) + len(corrs)

    def body(p_hbm, w_hbm, _, *refs):
        sources = [p_hbm.at[level] for level in projs] + [w_hbm.at[level] for level in corrs]
        sems = refs[-1]
        copies = [
            pltpu.make_async_copy(source, out, sems.at[at])
            for at, (source, out) in enumerate(zip(sources, refs[:-1]))
        ]
        for copy in copies:
            copy.start()
        for copy in copies:
            copy.wait()

    return pl.pallas_call(
        body,
        in_specs=[IN_HBM, IN_HBM, pl.BlockSpec(memory_space=pl.ANY)],
        out_specs=[IN_VMEM] * count,
        out_shape=[pltpu.VMEM((rows, rank), jnp.float32)] * count,
        scratch_shapes=[pltpu.SemaphoreType.DMA((count,))],
        compiler_params=pltpu.CompilerParams(vmem_limit_bytes=50 * MIB),
        cost_estimate=pl.CostEstimate(
            flops=0, bytes_accessed=2**16, transcendentals=0
        ),
        name="fetch",
    )(proj_bases, corr_bases, after)


def finish(state, corr, held):
    width, rows = state.shape

    def body(x_ref, w_ref, t_ref, out_ref):
        out_ref[...] = (x_ref[...] - three_passes(t_ref[...], w_ref[...], 1)).T

    return pl.pallas_call(
        body,
        in_specs=[IN_VMEM] * 3,
        out_specs=IN_VMEM,
        out_shape=jax.ShapeDtypeStruct((rows, width), jnp.float32),
        compiler_params=pltpu.CompilerParams(vmem_limit_bytes=16 * MIB),
        cost_estimate=pl.CostEstimate(
            flops=6 * rows * width * corr.shape[1], bytes_accessed=2**21, transcendentals=0
        ),
        name="finish",
    )(state, corr, held)


def on_device(rhs, proj_bases, corr_bases, cores):
    count = lax.axis_size("leaf")
    me = lax.axis_index("leaf")
    rows_here, width = rhs.shape
    rank = proj_bases.shape[2]
    bits = [(count >> level).bit_length() - 2 for level in range(LEVELS)]
    first = LEVELS - 1
    chain = [level for level in reversed(range(LEVELS)) if bits[level] > 0]

    parity = me & 1
    for bit in range(1, count.bit_length() - 1):
        parity = parity ^ ((me >> bit) & 1)
    lows = [(me >> bit) & 1 == 0 for bit in range(count.bit_length() - 1)]
    rhs, upper, *lows = lax.optimization_barrier((rhs, parity == 0, *lows))

    def low(bit):
        return lows[bit]

    def across(value, bit):
        return exchange(value, (1 << bit) | (1 if bit > 0 else 0))

    def chip_sum(value):
        half = width // 2
        keep = jnp.where(upper, value[:half], value[half:])
        send = jnp.where(upper, value[half:], value[:half])
        return keep + exchange(send, 1)

    def chip_gather(value):
        return pair_up(upper, value, exchange(value, 1), 0)

    heads = [(level, rank >> bits[level]) for level in chain if bits[level] == 1]
    tails = [(level, rank >> bits[level]) for level in chain if bits[level] > 1]
    near = [item for item in tails if heads and bits[item[0]] == 2]
    far = [item for item in tails if item not in near]
    groups = [group for group in (heads, near, far) if group]
    leaf_core = bits[first] == 0
    value, state, top_corr, next_proj, corr, proj, *fetched = begin(
        rhs, proj_bases, corr_bases, cores, first, leaf_core, groups
    )

    table = {}
    if leaf_core:
        table[first] = fetched.pop(0)

    def finish_table(level, mine):
        part = exchange(mine, 1)
        both = jnp.where(low(0), jnp.stack([mine, part], 1), jnp.stack([part, mine], 1))
        table[level] = both.reshape(rank, 2 * rank)

    def gather_steps(items, block, after):
        waiting = [level for level, _ in items]
        bit = 1
        coming = exchange(block if after is None else tie(block, after), 2)
        while True:
            after = yield
            block = pair_up(low(bit), block, tie(coming, after), 0)
            bit += 1
            after = yield
            rows = rank >> bit
            for level in [level for level in waiting if bits[level] == bit]:
                finish_table(level, tie(block[:, :rows], after))
                block = block[:, rows:]
            waiting = [level for level in waiting if bits[level] > bit]
            if not waiting:
                return
            after = yield
            coming = exchange(tie(block, after), 1 << bit)

    gathers = []

    def open_gather(items, block, after):
        steps = gather_steps(items, block[None], after)
        next(steps)
        gathers.append(steps)

    def step(after):
        try:
            gathers[0].send(after)
        except StopIteration:
            gathers.pop(0)

    if near:
        open_gather(near, fetched[1], None)
    else:
        open_gather(far, fetched[-1], None)

    def solve(level, value, ahead_of, later=None, fetch_rest=None):
        top = bits[level]
        for bit in range(1, top):
            value = ahead_of.get(bit, lambda v: v)(value)
            value = value + across(value, bit)
            if near and level < near[0][0] and bit == top - 2:
                step(value)
                step(value)
        if near and level == near[0][0]:
            open_gather(far, fetched[2], value)
        while level not in table:
            step(value)
        if fetch_rest is not None:
            later.append(fetch_rest(value))
        value = ahead_of.get(top, lambda v: v)(value)
        stacked = pair_up(low(top), value, across(value, top), 1)
        stacked = stacked / jnp.sqrt(jnp.float32(rows_here << top))
        return times_transposed(stacked, table[level])

    def update(corr, state, held):
        return state - jnp.einsum("ka,na->kn", held, corr, precision=HIGH)

    if leaf_core:
        top = pair_up(low(0), value, exchange(value, 1), 1)
        top = top / jnp.sqrt(jnp.float32(rows_here))
        held = times_transposed(top, table[first])
    else:
        held = chip_gather(solve(first, chip_sum(value), {}))
    state = update(top_corr, state, held)
    value = chip_sum(project(next_proj, state))
    if heads:
        finish_table(heads[0][0], tie(fetched[0], value)[None])
    later = []
    for level in reversed(range(1, first)):
        start = value
        if near and level == near[0][0]:
            step(start)
            step(start)
        elif near and level < near[0][0]:
            for _ in range(3):
                step(start)
        if level == first - 1:
            later.append(fetch(proj_bases, corr_bases, [level - 2], [level - 1], start))
        if level == first - 2:
            fetch_rest = lambda v: fetch(
                proj_bases, corr_bases, list(reversed(range(level - 1))), list(reversed(range(level))), v
            )
        held = solve(level, value, {}, later, fetch_rest if level == first - 2 else None)
        if level < first - 1:
            proj, corr = (later[0][0], later[0][1]) if level == first - 2 else (later[1][0], later[1][1])
        proj, corr = tie(proj, start), tie(corr, start)
        ahead = chip_sum(project(proj, state))
        own = jnp.einsum("na,nb->ab", proj, corr, precision=HIGH)
        value = ahead - times_transposed(held, own + exchange(own, 1))
        if level > 1:
            state = update(corr, state, chip_gather(held))
    gathered = chip_gather(held)
    state = update(corr, state, gathered)
    ahead_of = {bits[0]: lambda v: tie(v, state)}
    if near:
        step(value)
    held = solve(0, value, ahead_of)
    return finish(state, later[1][2], chip_gather(held))


def solution(mesh):
    return jax.shard_map(
        on_device,
        mesh=mesh,
        in_specs=(
            P("leaf", None),
            P(None, "leaf", None),
            P(None, "leaf", None),
            P(None, "leaf", None),
        ),
        out_specs=P("leaf", None),
        check_vma=False,
    )
```

```python
import jax
import jax.numpy as jnp
from jax import lax
from jax.experimental import pallas as pl
from jax.experimental.pallas import tpu as pltpu
from jax.sharding import PartitionSpec as P

LEVELS = 5
HIGH = lax.Precision.HIGH
MIB = 2**20
IN_HBM = pl.BlockSpec(memory_space=pltpu.HBM)
IN_VMEM = pl.BlockSpec(memory_space=pltpu.VMEM)


def exchange(value, mask):
    pairs = [(source, source ^ mask) for source in range(lax.axis_size("leaf"))]
    return lax.ppermute(value, "leaf", pairs)


def tie(value, after):
    return lax.optimization_barrier((value, after))[0]


def pair_up(low, mine, other, axis):
    return jnp.where(
        low,
        jnp.concatenate([mine, other], axis),
        jnp.concatenate([other, mine], axis),
    )


def project(basis, state):
    return jnp.einsum("kn,nr->kr", state, basis, precision=HIGH)


def times_transposed(left, right):
    return jnp.einsum("kb,ab->ka", left, right, precision=HIGH)


def parts(value):
    high = value.astype(jnp.bfloat16)
    return high, (value - high.astype(jnp.float32)).astype(jnp.bfloat16)


def three_passes(left, right, dim):
    rows = left.shape[0]
    left_high, left_low = parts(left)
    right_high, right_low = parts(right)

    def one(a, b):
        return lax.dot_general(a, b, (((1,), (dim,)), ((), ())), preferred_element_type=jnp.float32)

    both = one(jnp.concatenate([left_high, left_low], 0), right_high)
    return both[:rows] + (both[rows:] + one(left_high, right_low))


def begin(rhs, proj_bases, corr_bases, cores, first, leaf_core, groups):
    rows, width = rhs.shape
    rank = proj_bases.shape[2]
    shapes = [(width, rank), (width, rows)] + [(rows, rank)] * 4
    shapes += [(rank, 2 * rank)] if leaf_core else []
    shapes += [(sum(n for _, n in group), 2 * rank) for group in groups]

    def body(x_hbm, p_hbm, w_hbm, c_hbm, *refs):
        outs, (x_ref, p_ref, sems) = list(refs[: len(shapes)]), refs[len(shapes) :]
        q_out, state_out, w_out, p_out, w_next, p_next = outs[:6]
        rest = outs[6:]
        moves = [(x_hbm, x_ref), (p_hbm.at[first], p_ref)]
        if leaf_core:
            moves.append((c_hbm.at[first], rest.pop(0)))
        moves += [(w_hbm.at[first], w_out), (p_hbm.at[first - 1], p_out)]
        for group, out in zip(groups, rest):
            start = 0
            for level, n in group:
                moves.append((c_hbm.at[level, 0:n], out.at[start : start + n]))
                start += n
        moves += [(w_hbm.at[first - 1], w_next), (p_hbm.at[first - 2], p_next)]
        copies = [pltpu.make_async_copy(a, b, sems.at[at]) for at, (a, b) in enumerate(moves)]
        for copy in copies:
            copy.start()
        copies[0].wait()
        state = x_ref[...].T
        state_out[...] = state
        copies[1].wait()
        q_out[...] = three_passes(state, p_ref[...], 0)
        for copy in copies[2:]:
            copy.wait()

    count = 6 + (1 if leaf_core else 0) + sum(len(group) for group in groups)
    return pl.pallas_call(
        body,
        in_specs=[IN_HBM] * 4,
        out_specs=[IN_VMEM] * len(shapes),
        out_shape=[pltpu.VMEM(shape, jnp.float32) for shape in shapes],
        scratch_shapes=[
            pltpu.VMEM((rows, width), jnp.float32),
            pltpu.VMEM((rows, rank), jnp.float32),
            pltpu.SemaphoreType.DMA((count,)),
        ],
        compiler_params=pltpu.CompilerParams(vmem_limit_bytes=49 * MIB),
        cost_estimate=pl.CostEstimate(
            flops=6 * rows * width * rank, bytes_accessed=2**22, transcendentals=0
        ),
        name="begin",
    )(rhs, proj_bases, corr_bases, cores)


def fetch(proj_bases, corr_bases, projs, corrs, after):
    rows, rank = corr_bases.shape[1:]
    count = len(projs) + len(corrs)

    def body(p_hbm, w_hbm, _, *refs):
        sources = [p_hbm.at[level] for level in projs] + [w_hbm.at[level] for level in corrs]
        sems = refs[-1]
        copies = [
            pltpu.make_async_copy(source, out, sems.at[at])
            for at, (source, out) in enumerate(zip(sources, refs[:-1]))
        ]
        for copy in copies:
            copy.start()
        for copy in copies:
            copy.wait()

    return pl.pallas_call(
        body,
        in_specs=[IN_HBM, IN_HBM, pl.BlockSpec(memory_space=pl.ANY)],
        out_specs=[IN_VMEM] * count,
        out_shape=[pltpu.VMEM((rows, rank), jnp.float32)] * count,
        scratch_shapes=[pltpu.SemaphoreType.DMA((count,))],
        compiler_params=pltpu.CompilerParams(vmem_limit_bytes=50 * MIB),
        cost_estimate=pl.CostEstimate(
            flops=0, bytes_accessed=2**16, transcendentals=0
        ),
        name="fetch",
    )(proj_bases, corr_bases, after)


def finish(state, corr, held):
    width, rows = state.shape

    def body(x_ref, w_ref, t_ref, out_ref):
        out_ref[...] = (x_ref[...] - three_passes(t_ref[...], w_ref[...], 1)).T

    return pl.pallas_call(
        body,
        in_specs=[IN_VMEM] * 3,
        out_specs=IN_VMEM,
        out_shape=jax.ShapeDtypeStruct((rows, width), jnp.float32),
        compiler_params=pltpu.CompilerParams(vmem_limit_bytes=16 * MIB),
        cost_estimate=pl.CostEstimate(
            flops=6 * rows * width * corr.shape[1], bytes_accessed=2**21, transcendentals=0
        ),
        name="finish",
    )(state, corr, held)


def on_device(rhs, proj_bases, corr_bases, cores):
    count = lax.axis_size("leaf")
    me = lax.axis_index("leaf")
    rows_here, width = rhs.shape
    rank = proj_bases.shape[2]
    bits = [(count >> level).bit_length() - 2 for level in range(LEVELS)]
    first = LEVELS - 1
    chain = [level for level in reversed(range(LEVELS)) if bits[level] > 0]

    parity = me & 1
    for bit in range(1, count.bit_length() - 1):
        parity = parity ^ ((me >> bit) & 1)
    lows = [(me >> bit) & 1 == 0 for bit in range(count.bit_length() - 1)]
    rhs, upper, *lows = lax.optimization_barrier((rhs, parity == 0, *lows))

    def low(bit):
        return lows[bit]

    def across(value, bit):
        return exchange(value, (1 << bit) | (1 if bit > 0 else 0))

    def chip_sum(value):
        half = width // 2
        keep = jnp.where(upper, value[:half], value[half:])
        send = jnp.where(upper, value[half:], value[:half])
        return keep + exchange(send, 1)

    def chip_gather(value):
        return pair_up(upper, value, exchange(value, 1), 0)

    heads = [(level, rank >> bits[level]) for level in chain if bits[level] == 1]
    tails = [(level, rank >> bits[level]) for level in chain if bits[level] > 1]
    near = [item for item in tails if heads and bits[item[0]] == 2]
    far = [item for item in tails if item not in near]
    groups = [group for group in (heads, near, far) if group]
    leaf_core = bits[first] == 0
    value, state, top_corr, next_proj, corr, proj, *fetched = begin(
        rhs, proj_bases, corr_bases, cores, first, leaf_core, groups
    )

    table = {}
    if leaf_core:
        table[first] = fetched.pop(0)

    def finish_table(level, mine):
        part = exchange(mine, 1)
        both = jnp.where(low(0), jnp.stack([mine, part], 1), jnp.stack([part, mine], 1))
        table[level] = both.reshape(rank, 2 * rank)

    def gather_steps(items, block, after):
        waiting = [level for level, _ in items]
        bit = 1
        coming = exchange(block if after is None else tie(block, after), 2)
        while True:
            after = yield
            block = pair_up(low(bit), block, tie(coming, after), 0)
            bit += 1
            after = yield
            rows = rank >> bit
            for level in [level for level in waiting if bits[level] == bit]:
                finish_table(level, tie(block[:, :rows], after))
                block = block[:, rows:]
            waiting = [level for level in waiting if bits[level] > bit]
            if not waiting:
                return
            after = yield
            coming = exchange(tie(block, after), 1 << bit)

    gathers = []

    def open_gather(items, block, after):
        steps = gather_steps(items, block[None], after)
        next(steps)
        gathers.append(steps)

    def step(after):
        try:
            gathers[0].send(after)
        except StopIteration:
            gathers.pop(0)

    if near:
        open_gather(near, fetched[1], None)
    else:
        open_gather(far, fetched[-1], None)

    def solve(level, value, ahead_of, later=None, fetch_rest=None):
        top = bits[level]
        for bit in range(1, top):
            value = ahead_of.get(bit, lambda v: v)(value)
            value = value + across(value, bit)
            if near and level == 0 and bit == top - 2:
                step(value)
                step(value)
        if near and level == near[0][0]:
            open_gather(far, fetched[2], value)
        while level not in table:
            step(value)
        if fetch_rest is not None:
            later.append(fetch_rest(value))
        value = ahead_of.get(top, lambda v: v)(value)
        stacked = pair_up(low(top), value, across(value, top), 1)
        stacked = stacked / jnp.sqrt(jnp.float32(rows_here << top))
        return times_transposed(stacked, table[level])

    def update(corr, state, held):
        return state - jnp.einsum("ka,na->kn", held, corr, precision=HIGH)

    if leaf_core:
        top = pair_up(low(0), value, exchange(value, 1), 1)
        top = top / jnp.sqrt(jnp.float32(rows_here))
        held = times_transposed(top, table[first])
    else:
        held = chip_gather(solve(first, chip_sum(value), {}))
    state = update(top_corr, state, held)
    value = chip_sum(project(next_proj, state))
    if heads:
        finish_table(heads[0][0], tie(fetched[0], value)[None])
    later = []
    for level in reversed(range(1, first)):
        start = value
        if near and level == near[0][0]:
            step(start)
            step(start)
        elif near and level < near[0][0]:
            for _ in range(3):
                step(start)
        if level == first - 1:
            later.append(fetch(proj_bases, corr_bases, [level - 2], [level - 1], start))
        if level == first - 2:
            fetch_rest = lambda v: fetch(
                proj_bases, corr_bases, list(reversed(range(level - 1))), list(reversed(range(level))), v
            )
        held = solve(level, value, {}, later, fetch_rest if level == first - 2 else None)
        if level < first - 1:
            proj, corr = (later[0][0], later[0][1]) if level == first - 2 else (later[1][0], later[1][1])
        proj, corr = tie(proj, start), tie(corr, start)
        ahead = chip_sum(project(proj, state))
        own = jnp.einsum("na,nb->ab", proj, corr, precision=HIGH)
        value = ahead - times_transposed(held, own + exchange(own, 1))
        if level > 1:
            state = update(corr, state, chip_gather(held))
    gathered = chip_gather(held)
    state = update(corr, state, gathered)
    ahead_of = {bits[0]: lambda v: tie(v, state)}
    if near:
        step(value)
    held = solve(0, value, ahead_of)
    return finish(state, later[1][2], chip_gather(held))


def solution(mesh):
    return jax.shard_map(
        on_device,
        mesh=mesh,
        in_specs=(
            P("leaf", None),
            P(None, "leaf", None),
            P(None, "leaf", None),
            P(None, "leaf", None),
        ),
        out_specs=P("leaf", None),
        check_vma=False,
    )
```

```python
import jax
import jax.numpy as jnp
from jax import lax
from jax.experimental import pallas as pl
from jax.experimental.pallas import tpu as pltpu
from jax.sharding import PartitionSpec as P

LEVELS = 5
HIGH = lax.Precision.HIGH
MIB = 2**20
IN_HBM = pl.BlockSpec(memory_space=pltpu.HBM)
IN_VMEM = pl.BlockSpec(memory_space=pltpu.VMEM)


def exchange(value, mask):
    pairs = [(source, source ^ mask) for source in range(lax.axis_size("leaf"))]
    return lax.ppermute(value, "leaf", pairs)


def tie(value, after):
    return lax.optimization_barrier((value, after))[0]


def pair_up(low, mine, other, axis):
    return jnp.where(
        low,
        jnp.concatenate([mine, other], axis),
        jnp.concatenate([other, mine], axis),
    )


def project(basis, state):
    return jnp.einsum("kn,nr->kr", state, basis, precision=HIGH)


def times_transposed(left, right):
    return jnp.einsum("kb,ab->ka", left, right, precision=HIGH)


def parts(value):
    high = value.astype(jnp.bfloat16)
    return high, (value - high.astype(jnp.float32)).astype(jnp.bfloat16)


def three_passes(left, right, dim):
    rows = left.shape[0]
    left_high, left_low = parts(left)
    right_high, right_low = parts(right)

    def one(a, b):
        return lax.dot_general(a, b, (((1,), (dim,)), ((), ())), preferred_element_type=jnp.float32)

    both = one(jnp.concatenate([left_high, left_low], 0), right_high)
    return both[:rows] + (both[rows:] + one(left_high, right_low))


def begin(rhs, proj_bases, corr_bases, cores, first, leaf_core, groups):
    rows, width = rhs.shape
    rank = proj_bases.shape[2]
    shapes = [(width, rank), (width, rows)] + [(rows, rank)] * 4
    shapes += [(rank, 2 * rank)] if leaf_core else []
    shapes += [(sum(n for _, n in group), 2 * rank) for group in groups]

    def body(x_hbm, p_hbm, w_hbm, c_hbm, *refs):
        outs, (x_ref, p_ref, sems) = list(refs[: len(shapes)]), refs[len(shapes) :]
        q_out, state_out, w_out, p_out, w_next, p_next = outs[:6]
        rest = outs[6:]
        moves = [(x_hbm, x_ref), (p_hbm.at[first], p_ref)]
        if leaf_core:
            moves.append((c_hbm.at[first], rest.pop(0)))
        moves += [(w_hbm.at[first], w_out), (p_hbm.at[first - 1], p_out)]
        for group, out in zip(groups, rest):
            start = 0
            for level, n in group:
                moves.append((c_hbm.at[level, 0:n], out.at[start : start + n]))
                start += n
        moves += [(w_hbm.at[first - 1], w_next), (p_hbm.at[first - 2], p_next)]
        copies = [pltpu.make_async_copy(a, b, sems.at[at]) for at, (a, b) in enumerate(moves)]
        for copy in copies:
            copy.start()
        copies[0].wait()
        state = x_ref[...].T
        state_out[...] = state
        copies[1].wait()
        q_out[...] = three_passes(state, p_ref[...], 0)
        for copy in copies[2:]:
            copy.wait()

    count = 6 + (1 if leaf_core else 0) + sum(len(group) for group in groups)
    return pl.pallas_call(
        body,
        in_specs=[IN_HBM] * 4,
        out_specs=[IN_VMEM] * len(shapes),
        out_shape=[pltpu.VMEM(shape, jnp.float32) for shape in shapes],
        scratch_shapes=[
            pltpu.VMEM((rows, width), jnp.float32),
            pltpu.VMEM((rows, rank), jnp.float32),
            pltpu.SemaphoreType.DMA((count,)),
        ],
        compiler_params=pltpu.CompilerParams(vmem_limit_bytes=49 * MIB),
        cost_estimate=pl.CostEstimate(
            flops=6 * rows * width * rank, bytes_accessed=2**22, transcendentals=0
        ),
        name="begin",
    )(rhs, proj_bases, corr_bases, cores)


def fetch(proj_bases, corr_bases, projs, corrs, after):
    rows, rank = corr_bases.shape[1:]
    count = len(projs) + len(corrs)

    def body(p_hbm, w_hbm, _, *refs):
        sources = [p_hbm.at[level] for level in projs] + [w_hbm.at[level] for level in corrs]
        sems = refs[-1]
        copies = [
            pltpu.make_async_copy(source, out, sems.at[at])
            for at, (source, out) in enumerate(zip(sources, refs[:-1]))
        ]
        for copy in copies:
            copy.start()
        for copy in copies:
            copy.wait()

    return pl.pallas_call(
        body,
        in_specs=[IN_HBM, IN_HBM, pl.BlockSpec(memory_space=pl.ANY)],
        out_specs=[IN_VMEM] * count,
        out_shape=[pltpu.VMEM((rows, rank), jnp.float32)] * count,
        scratch_shapes=[pltpu.SemaphoreType.DMA((count,))],
        compiler_params=pltpu.CompilerParams(vmem_limit_bytes=50 * MIB),
        cost_estimate=pl.CostEstimate(
            flops=0, bytes_accessed=2**16, transcendentals=0
        ),
        name="fetch",
    )(proj_bases, corr_bases, after)


def finish(state, corr, held):
    width, rows = state.shape

    def body(x_ref, w_ref, t_ref, out_ref):
        out_ref[...] = (x_ref[...] - three_passes(t_ref[...], w_ref[...], 1)).T

    return pl.pallas_call(
        body,
        in_specs=[IN_VMEM] * 3,
        out_specs=IN_VMEM,
        out_shape=jax.ShapeDtypeStruct((rows, width), jnp.float32),
        compiler_params=pltpu.CompilerParams(vmem_limit_bytes=16 * MIB),
        cost_estimate=pl.CostEstimate(
            flops=6 * rows * width * corr.shape[1], bytes_accessed=2**21, transcendentals=0
        ),
        name="finish",
    )(state, corr, held)


def on_device(rhs, proj_bases, corr_bases, cores):
    count = lax.axis_size("leaf")
    me = lax.axis_index("leaf")
    rows_here, width = rhs.shape
    rank = proj_bases.shape[2]
    bits = [(count >> level).bit_length() - 2 for level in range(LEVELS)]
    first = LEVELS - 1
    chain = [level for level in reversed(range(LEVELS)) if bits[level] > 0]

    parity = me & 1
    for bit in range(1, count.bit_length() - 1):
        parity = parity ^ ((me >> bit) & 1)
    lows = [(me >> bit) & 1 == 0 for bit in range(count.bit_length() - 1)]
    rhs, upper, *lows = lax.optimization_barrier((rhs, parity == 0, *lows))

    def low(bit):
        return lows[bit]

    def across(value, bit):
        return exchange(value, (1 << bit) | (1 if bit > 0 else 0))

    def chip_sum(value):
        half = width // 2
        keep = jnp.where(upper, value[:half], value[half:])
        send = jnp.where(upper, value[half:], value[:half])
        return keep + exchange(send, 1)

    def chip_gather(value):
        return pair_up(upper, value, exchange(value, 1), 0)

    heads = [(level, rank >> bits[level]) for level in chain if bits[level] == 1]
    tails = [(level, rank >> bits[level]) for level in chain if bits[level] > 1]
    near = [item for item in tails if heads and bits[item[0]] == 2]
    far = [item for item in tails if item not in near]
    groups = [group for group in (heads, near, far) if group]
    leaf_core = bits[first] == 0
    value, state, top_corr, next_proj, corr, proj, *fetched = begin(
        rhs, proj_bases, corr_bases, cores, first, leaf_core, groups
    )

    table = {}
    if leaf_core:
        table[first] = fetched.pop(0)

    def finish_table(level, mine):
        part = exchange(mine, 1)
        both = jnp.where(low(0), jnp.stack([mine, part], 1), jnp.stack([part, mine], 1))
        table[level] = both.reshape(rank, 2 * rank)

    def gather_steps(items, block, after):
        waiting = [level for level, _ in items]
        bit = 1
        coming = exchange(block if after is None else tie(block, after), 2)
        while True:
            after = yield
            block = pair_up(low(bit), block, tie(coming, after), 0)
            bit += 1
            after = yield
            rows = rank >> bit
            for level in [level for level in waiting if bits[level] == bit]:
                finish_table(level, tie(block[:, :rows], after))
                block = block[:, rows:]
            waiting = [level for level in waiting if bits[level] > bit]
            if not waiting:
                return
            after = yield
            coming = exchange(tie(block, after), 1 << bit)

    gathers = []

    def open_gather(items, block, after):
        steps = gather_steps(items, block[None], after)
        next(steps)
        gathers.append(steps)

    def step(after):
        try:
            gathers[0].send(after)
        except StopIteration:
            gathers.pop(0)

    if near:
        open_gather(near, fetched[1], None)
    else:
        open_gather(far, fetched[-1], None)

    marks = {}

    def solve(level, value, ahead_of, later=None, fetch_rest=None):
        top = bits[level]
        for bit in range(1, top):
            value = ahead_of.get(bit, lambda v: v)(value)
            value = value + across(value, bit)
            if bit == 1:
                marks[level] = value
            if near and level == 0 and bit == top - 2:
                step(value)
                step(value)
        if near and level == near[0][0]:
            open_gather(far, fetched[2], value)
        while level not in table:
            step(value)
        if fetch_rest is not None:
            later.append(fetch_rest(value))
        value = ahead_of.get(top, lambda v: v)(value)
        stacked = pair_up(low(top), value, across(value, top), 1)
        stacked = stacked / jnp.sqrt(jnp.float32(rows_here << top))
        return times_transposed(stacked, table[level])

    def update(corr, state, held):
        return state - jnp.einsum("ka,na->kn", held, corr, precision=HIGH)

    if leaf_core:
        top = pair_up(low(0), value, exchange(value, 1), 1)
        top = top / jnp.sqrt(jnp.float32(rows_here))
        held = times_transposed(top, table[first])
    else:
        held = chip_gather(solve(first, chip_sum(value), {}))
    state = update(top_corr, state, held)
    value = chip_sum(project(next_proj, state))
    if heads:
        finish_table(heads[0][0], tie(fetched[0], value)[None])
    later = []
    for level in reversed(range(1, first)):
        start = value
        if near and level == near[0][0]:
            step(start)
            step(start)
        elif near and level < near[0][0]:
            for _ in range(3):
                step(start)
        if level == first - 1:
            later.append(fetch(proj_bases, corr_bases, [level - 2], [level - 1], start))
        if level == first - 2:
            fetch_rest = lambda v: fetch(
                proj_bases, corr_bases, list(reversed(range(level - 1))), list(reversed(range(level))), v
            )
        held = solve(level, value, {}, later, fetch_rest if level == first - 2 else None)
        if level < first - 1:
            proj, corr = (later[0][0], later[0][1]) if level == first - 2 else (later[1][0], later[1][1])
        after = marks[level] if level == 1 else start
        proj, corr = tie(proj, after), tie(corr, after)
        ahead = chip_sum(project(proj, state))
        own = jnp.einsum("na,nb->ab", proj, corr, precision=HIGH)
        value = ahead - times_transposed(held, own + exchange(own, 1))
        if level > 1:
            state = update(corr, state, chip_gather(held))
    gathered = chip_gather(held)
    state = update(corr, state, gathered)
    ahead_of = {bits[0]: lambda v: tie(v, state)}
    if near:
        step(value)
    held = solve(0, value, ahead_of)
    return finish(state, later[1][2], chip_gather(held))


def solution(mesh):
    return jax.shard_map(
        on_device,
        mesh=mesh,
        in_specs=(
            P("leaf", None),
            P(None, "leaf", None),
            P(None, "leaf", None),
            P(None, "leaf", None),
        ),
        out_specs=P("leaf", None),
        check_vma=False,
    )
```

```python
import jax
import jax.numpy as jnp
from jax import lax
from jax.experimental import pallas as pl
from jax.experimental.pallas import tpu as pltpu
from jax.sharding import PartitionSpec as P

LEVELS = 5
HIGH = lax.Precision.HIGH
MIB = 2**20
IN_HBM = pl.BlockSpec(memory_space=pltpu.HBM)
IN_VMEM = pl.BlockSpec(memory_space=pltpu.VMEM)


def exchange(value, mask):
    pairs = [(source, source ^ mask) for source in range(lax.axis_size("leaf"))]
    return lax.ppermute(value, "leaf", pairs)


def tie(value, after):
    return lax.optimization_barrier((value, after))[0]


def pair_up(low, mine, other, axis):
    return jnp.where(
        low,
        jnp.concatenate([mine, other], axis),
        jnp.concatenate([other, mine], axis),
    )


def project(basis, state):
    return jnp.einsum("kn,nr->kr", state, basis, precision=HIGH)


def times_transposed(left, right):
    return jnp.einsum("kb,ab->ka", left, right, precision=HIGH)


def parts(value):
    high = value.astype(jnp.bfloat16)
    return high, (value - high.astype(jnp.float32)).astype(jnp.bfloat16)


def three_passes(left, right, dim):
    rows = left.shape[0]
    left_high, left_low = parts(left)
    right_high, right_low = parts(right)

    def one(a, b):
        return lax.dot_general(a, b, (((1,), (dim,)), ((), ())), preferred_element_type=jnp.float32)

    both = one(jnp.concatenate([left_high, left_low], 0), right_high)
    return both[:rows] + (both[rows:] + one(left_high, right_low))


def begin(rhs, proj_bases, corr_bases, cores, first, leaf_core, groups):
    rows, width = rhs.shape
    rank = proj_bases.shape[2]
    shapes = [(width, rank), (width, rows)] + [(rows, rank)] * 6
    shapes += [(rank, 2 * rank)] if leaf_core else []
    shapes += [(sum(n for _, n in group), 2 * rank) for group in groups]

    def body(x_hbm, p_hbm, w_hbm, c_hbm, *refs):
        outs, (x_ref, p_ref, sems) = list(refs[: len(shapes)]), refs[len(shapes) :]
        q_out, state_out, w_out, p_out, w_next, p_next, w_third, p_third = outs[:8]
        rest = outs[8:]
        moves = [(x_hbm, x_ref), (p_hbm.at[first], p_ref)]
        if leaf_core:
            moves.append((c_hbm.at[first], rest.pop(0)))
        moves += [(w_hbm.at[first], w_out), (p_hbm.at[first - 1], p_out)]
        for group, out in zip(groups, rest):
            start = 0
            for level, n in group:
                moves.append((c_hbm.at[level, 0:n], out.at[start : start + n]))
                start += n
        moves += [(w_hbm.at[first - 1], w_next), (p_hbm.at[first - 2], p_next)]
        moves += [(w_hbm.at[first - 2], w_third), (p_hbm.at[first - 3], p_third)]
        copies = [pltpu.make_async_copy(a, b, sems.at[at]) for at, (a, b) in enumerate(moves)]
        for copy in copies:
            copy.start()
        copies[0].wait()
        state = x_ref[...].T
        state_out[...] = state
        copies[1].wait()
        q_out[...] = three_passes(state, p_ref[...], 0)
        for copy in copies[2:]:
            copy.wait()

    count = 8 + (1 if leaf_core else 0) + sum(len(group) for group in groups)
    return pl.pallas_call(
        body,
        in_specs=[IN_HBM] * 4,
        out_specs=[IN_VMEM] * len(shapes),
        out_shape=[pltpu.VMEM(shape, jnp.float32) for shape in shapes],
        scratch_shapes=[
            pltpu.VMEM((rows, width), jnp.float32),
            pltpu.VMEM((rows, rank), jnp.float32),
            pltpu.SemaphoreType.DMA((count,)),
        ],
        compiler_params=pltpu.CompilerParams(vmem_limit_bytes=49 * MIB),
        cost_estimate=pl.CostEstimate(
            flops=6 * rows * width * rank, bytes_accessed=2**22, transcendentals=0
        ),
        name="begin",
    )(rhs, proj_bases, corr_bases, cores)


def fetch(proj_bases, corr_bases, projs, corrs, after):
    rows, rank = corr_bases.shape[1:]
    count = len(projs) + len(corrs)

    def body(p_hbm, w_hbm, _, *refs):
        sources = [p_hbm.at[level] for level in projs] + [w_hbm.at[level] for level in corrs]
        sems = refs[-1]
        copies = [
            pltpu.make_async_copy(source, out, sems.at[at])
            for at, (source, out) in enumerate(zip(sources, refs[:-1]))
        ]
        for copy in copies:
            copy.start()
        for copy in copies:
            copy.wait()

    return pl.pallas_call(
        body,
        in_specs=[IN_HBM, IN_HBM, pl.BlockSpec(memory_space=pl.ANY)],
        out_specs=[IN_VMEM] * count,
        out_shape=[pltpu.VMEM((rows, rank), jnp.float32)] * count,
        scratch_shapes=[pltpu.SemaphoreType.DMA((count,))],
        compiler_params=pltpu.CompilerParams(vmem_limit_bytes=50 * MIB),
        cost_estimate=pl.CostEstimate(
            flops=0, bytes_accessed=2**16, transcendentals=0
        ),
        name="fetch",
    )(proj_bases, corr_bases, after)


def finish(state, corr, held):
    width, rows = state.shape

    def body(x_ref, w_ref, t_ref, out_ref):
        out_ref[...] = (x_ref[...] - three_passes(t_ref[...], w_ref[...], 1)).T

    return pl.pallas_call(
        body,
        in_specs=[IN_VMEM] * 3,
        out_specs=IN_VMEM,
        out_shape=jax.ShapeDtypeStruct((rows, width), jnp.float32),
        compiler_params=pltpu.CompilerParams(vmem_limit_bytes=16 * MIB),
        cost_estimate=pl.CostEstimate(
            flops=6 * rows * width * corr.shape[1], bytes_accessed=2**21, transcendentals=0
        ),
        name="finish",
    )(state, corr, held)


def on_device(rhs, proj_bases, corr_bases, cores):
    count = lax.axis_size("leaf")
    me = lax.axis_index("leaf")
    rows_here, width = rhs.shape
    rank = proj_bases.shape[2]
    bits = [(count >> level).bit_length() - 2 for level in range(LEVELS)]
    first = LEVELS - 1
    chain = [level for level in reversed(range(LEVELS)) if bits[level] > 0]

    parity = me & 1
    for bit in range(1, count.bit_length() - 1):
        parity = parity ^ ((me >> bit) & 1)
    lows = [(me >> bit) & 1 == 0 for bit in range(count.bit_length() - 1)]
    rhs, upper, *lows = lax.optimization_barrier((rhs, parity == 0, *lows))

    def low(bit):
        return lows[bit]

    def across(value, bit):
        return exchange(value, (1 << bit) | (1 if bit > 0 else 0))

    def chip_sum(value):
        half = width // 2
        keep = jnp.where(upper, value[:half], value[half:])
        send = jnp.where(upper, value[half:], value[:half])
        return keep + exchange(send, 1)

    def chip_gather(value):
        return pair_up(upper, value, exchange(value, 1), 0)

    heads = [(level, rank >> bits[level]) for level in chain if bits[level] == 1]
    tails = [(level, rank >> bits[level]) for level in chain if bits[level] > 1]
    near = [item for item in tails if heads and bits[item[0]] == 2]
    far = [item for item in tails if item not in near]
    groups = [group for group in (heads, near, far) if group]
    leaf_core = bits[first] == 0
    value, state, top_corr, next_proj, corr, proj, third_corr, third_proj, *fetched = begin(
        rhs, proj_bases, corr_bases, cores, first, leaf_core, groups
    )

    table = {}
    if leaf_core:
        table[first] = fetched.pop(0)

    def finish_table(level, mine):
        part = exchange(mine, 1)
        both = jnp.where(low(0), jnp.stack([mine, part], 1), jnp.stack([part, mine], 1))
        table[level] = both.reshape(rank, 2 * rank)

    def gather_steps(items, block, after):
        waiting = [level for level, _ in items]
        bit = 1
        coming = exchange(block if after is None else tie(block, after), 2)
        while True:
            after = yield
            block = pair_up(low(bit), block, tie(coming, after), 0)
            bit += 1
            after = yield
            rows = rank >> bit
            for level in [level for level in waiting if bits[level] == bit]:
                finish_table(level, tie(block[:, :rows], after))
                block = block[:, rows:]
            waiting = [level for level in waiting if bits[level] > bit]
            if not waiting:
                return
            after = yield
            coming = exchange(tie(block, after), 1 << bit)

    gathers = []

    def open_gather(items, block, after):
        steps = gather_steps(items, block[None], after)
        next(steps)
        gathers.append(steps)

    def step(after):
        try:
            gathers[0].send(after)
        except StopIteration:
            gathers.pop(0)

    if near:
        open_gather(near, fetched[1], None)
    else:
        open_gather(far, fetched[-1], None)

    marks = {}

    def solve(level, value, ahead_of, later=None, fetch_rest=None):
        top = bits[level]
        for bit in range(1, top):
            value = ahead_of.get(bit, lambda v: v)(value)
            value = value + across(value, bit)
            if bit == 1:
                marks[level] = value
            if near and level == 0 and bit == top - 2:
                step(value)
                step(value)
        if near and level == near[0][0]:
            open_gather(far, fetched[2], value)
        while level not in table:
            step(value)
        if fetch_rest is not None:
            later.append(fetch_rest(value))
        value = ahead_of.get(top, lambda v: v)(value)
        stacked = pair_up(low(top), value, across(value, top), 1)
        stacked = stacked / jnp.sqrt(jnp.float32(rows_here << top))
        return times_transposed(stacked, table[level])

    def update(corr, state, held):
        return state - jnp.einsum("ka,na->kn", held, corr, precision=HIGH)

    if leaf_core:
        top = pair_up(low(0), value, exchange(value, 1), 1)
        top = top / jnp.sqrt(jnp.float32(rows_here))
        held = times_transposed(top, table[first])
    else:
        held = chip_gather(solve(first, chip_sum(value), {}))
    state = update(top_corr, state, held)
    value = chip_sum(project(next_proj, state))
    if heads:
        finish_table(heads[0][0], tie(fetched[0], value)[None])
    later = []
    for level in reversed(range(1, first)):
        start = value
        if near and level == near[0][0]:
            step(start)
            step(start)
        elif near and level < near[0][0]:
            for _ in range(3):
                step(start)
        if level == first - 1:
            later.append((third_proj, third_corr))
        if level == first - 2:
            fetch_rest = lambda v: fetch(
                proj_bases, corr_bases, list(reversed(range(level - 1))), list(reversed(range(level))), v
            )
        held = solve(level, value, {}, later, fetch_rest if level == first - 2 else None)
        if level < first - 1:
            proj, corr = (later[0][0], later[0][1]) if level == first - 2 else (later[1][0], later[1][1])
        after = marks[level] if level == 1 else start
        proj, corr = tie(proj, after), tie(corr, after)
        ahead = chip_sum(project(proj, state))
        own = jnp.einsum("na,nb->ab", proj, corr, precision=HIGH)
        value = ahead - times_transposed(held, own + exchange(own, 1))
        if level > 1:
            state = update(corr, state, chip_gather(held))
    gathered = chip_gather(held)
    state = update(corr, state, gathered)
    ahead_of = {bits[0]: lambda v: tie(v, state)}
    if near:
        step(value)
    held = solve(0, value, ahead_of)
    return finish(state, later[1][2], chip_gather(held))


def solution(mesh):
    return jax.shard_map(
        on_device,
        mesh=mesh,
        in_specs=(
            P("leaf", None),
            P(None, "leaf", None),
            P(None, "leaf", None),
            P(None, "leaf", None),
        ),
        out_specs=P("leaf", None),
        check_vma=False,
    )
```
